128 devices in a mesh: shot: 8 (over y, core), tile: 16 (over z, x).
Axes of the slice: x: 4, y: 4, z: 4, core: 2. Of those that a mesh axis runs over, the one named last changes fastest.
Arguments:
- coefs: float32 [3, 16, 2048, 128], P(None, 'shot', 'tile')
- fwd_state: float32 [8, 4, 16, 2048, 128], P('shot', None, None, 'tile'), may hold values from -3 to 3
- adj_state: float32 [8, 4, 16, 2048, 128], P('shot', None, None, 'tile'), may hold values from -3 to 3
- src_cell: int32 [8, 16], P('shot', 'tile'), may hold values from 0 to 262143
- src_wave: float32 [8, 6], P('shot'), may hold values from -8 to 8
- rec_cells: int32 [8, 2048], P('shot', 'tile'), may hold values from 0 to 262143
- observed: float32 [8, 6, 2048], P('shot', None, 'tile'), may hold values from -6 to 6
Outputs:
- gradient: float32 [3, 16, 2048, 128], P(None, 'shot', 'tile')
- fwd_final: float32 [8, 2, 16, 2048, 128], P('shot', None, None, 'tile')
- adj_final: float32 [8, 2, 16, 2048, 128], P('shot', None, None, 'tile')
The draws below stay inside these ranges and needn't reach their ends.
Inputs may be any that keep to these rules, and one draw needn't show every extreme that they name: `src_cell`: local cell index depth * 128 * 128 + first * 128 + second inside the aperture tile. `rec_cells`: local cell index inside the tile of the receiver's block; cells may repeat.
All inputs are finite; a program needn't handle non-finite values.
Results may differ from the reference program's by a relative error of at most 0.0003.
Values sent between devices are 32-bit elements; how exact they have to be, the bound alone decides.
A program may use at most 192 MiB of HBM per device.

```python
import jax
import jax.numpy as jnp
from jax import lax

AX = 128
AY = 128
AZ = 16
STEPS = 6
NREC = 128
NX = 2048
N_SHOT = 8
N_TILE = 16


def draw_coefs(key, part):
    shape = (AZ, AX * N_TILE, AY)
    keys = jax.random.split(jax.random.fold_in(key, 17), 3)
    speed = jax.random.uniform(keys[0], shape, jnp.float32, 0.03, 0.15)
    stretch = jax.random.uniform(keys[1], shape, jnp.float32, 1.2, 1.6)
    couple = jax.random.uniform(keys[2], shape, jnp.float32, 0.9, 1.05)
    return jnp.stack([speed, stretch, couple])


def touch_ends(result, rng, low, top_value):
    dims = result.shape
    place = [jax.random.randint(jax.random.fold_in(rng, axis), (), 0, dims[axis]) for axis in range(len(dims))]
    result = result.at[tuple(place)].set(low)
    longest = dims.index(max(dims))
    place[longest] = (place[longest] + 1) % dims[longest]
    return result.at[tuple(place)].set(top_value)


def block_levels(rng, dims, pieces, low, largest):
    def one(axis_at, parts):
        draws = jax.random.uniform(jax.random.fold_in(jax.random.fold_in(rng, 6), axis_at), (parts,), jnp.float32, low / len(pieces), largest / len(pieces))
        return jnp.repeat(jnp.exp(draws), dims[axis_at] // parts).reshape((-1,) + (1,) * (len(dims) - axis_at - 1))

    loudness = one(*pieces[0])
    for cut in pieces[1:]:
        loudness = loudness * one(*cut)
    return loudness


def gaussian(own_key, dims, scale, most, cuts=(), kind=jnp.bfloat16):
    level = block_levels(own_key, dims, cuts, -0.22, 0.18) if cuts else 1.0
    drawn = jax.random.normal(own_key, dims, jnp.float32) * scale * level
    return jnp.minimum(jnp.maximum(drawn, -most), most).astype(kind)


def setup_inputs(seed: int = 0) -> dict:
    key_of = jax.random.split(jax.random.key(seed), 8)
    return {
        "coefs": draw_coefs(jax.random.fold_in(key_of[7], 71), 0),
        "fwd_state": gaussian(key_of[1], (N_SHOT, 4, AZ, NX, AY), 0.5, 3.0, ((0, 8), (3, 16)), jnp.float32),
        "adj_state": gaussian(key_of[2], (N_SHOT, 4, AZ, NX, AY), 0.5, 3.0, ((0, 8), (3, 16)), jnp.float32),
        "src_cell": touch_ends(jax.random.randint(key_of[3], (N_SHOT, N_TILE), 0, AZ * AX * AY), jax.random.fold_in(key_of[3], 1), 0, (AZ * AX * AY) - 1).astype(jnp.int32),
        "src_wave": gaussian(key_of[4], (N_SHOT, STEPS), 2.0, 8.0, ((0, 8),), jnp.float32),
        "rec_cells": touch_ends(jax.random.randint(key_of[5], (N_SHOT, N_TILE * NREC), 0, AZ * AX * AY), jax.random.fold_in(key_of[5], 1), 0, (AZ * AX * AY) - 1).astype(jnp.int32),
        "observed": gaussian(key_of[6], (N_SHOT, STEPS, N_TILE * NREC), 1.0, 6.0, ((0, 8), (2, 16)), jnp.float32),
    }


def second_diff(field, axis):
    pads = [(0, 0), (0, 0), (0, 0)]
    pads[axis] = (2, 2)
    padded = jnp.pad(field, pads)
    size = field.shape[axis]

    def part(k):
        return lax.slice_in_dim(padded, k, k + size, axis=axis)

    return (-part(0) + 16.0 * part(1) - 30.0 * part(2) + 16.0 * part(3) - part(4)) / 12.0


def global_index(local, tile_of):
    depth = local // (AX * AY)
    first = tile_of * AX + (local // AY) % AX
    second = local % AY
    return ((depth * NX + first) * AY + second).astype(jnp.int32)


def reference(coefs, fwd_state, adj_state, src_cell, src_wave, rec_cells, observed):
    speed, stretch, couple = coefs[0], coefs[1], coefs[2]
    shape = speed.shape
    cells = AZ * NX * AY
    tiles_src = jnp.arange(N_TILE, dtype=jnp.int32)
    tiles_rec = (jnp.arange(N_TILE * NREC, dtype=jnp.int32) // NREC).astype(jnp.int32)
    grad_total = jnp.zeros((3,) + shape, jnp.float32)
    fwd_out = []
    adj_out = []
    for shot in range(N_SHOT):
        src_idx = global_index(src_cell[shot], tiles_src)
        rec_idx = global_index(rec_cells[shot], tiles_rec)
        upper, lower, upper_old, lower_old = fwd_state[shot, 0], fwd_state[shot, 1], fwd_state[shot, 2], fwd_state[shot, 3]
        stored = []
        records = []
        for step in range(STEPS):
            horiz = second_diff(upper, 1) + second_diff(upper, 2)
            vert = second_diff(lower, 0)
            pulse = jnp.zeros((cells,), jnp.float32).at[src_idx].add(src_wave[shot, step]).reshape(shape)
            upper_next = 2.0 * upper - upper_old + speed * (stretch * horiz + couple * vert) + pulse
            lower_next = 2.0 * lower - lower_old + speed * (couple * horiz + vert) + pulse
            stored.append((horiz, vert))
            records.append(upper_next.reshape(-1)[rec_idx] - observed[shot, step])
            upper_old, lower_old, upper, lower = upper, lower, upper_next, lower_next
        fwd_out.append(jnp.stack([upper, lower]))
        lam, mu, lam_old, mu_old = adj_state[shot, 0], adj_state[shot, 1], adj_state[shot, 2], adj_state[shot, 3]
        acc_h = jnp.zeros(shape, jnp.float32)
        acc_x = jnp.zeros(shape, jnp.float32)
        acc_z = jnp.zeros(shape, jnp.float32)
        for step in reversed(range(STEPS)):
            first = speed * (stretch * lam + couple * mu)
            other = speed * (couple * lam + mu)
            inject = jnp.zeros((cells,), jnp.float32).at[rec_idx].add(records[step]).reshape(shape)
            lam_new = inject + 2.0 * lam + (second_diff(first, 1) + second_diff(first, 2)) - lam_old
            mu_new = 2.0 * mu + second_diff(other, 0) - mu_old
            horiz, vert = stored[step]
            acc_h = acc_h + lam_new * horiz
            acc_x = acc_x + lam_new * vert + mu_new * horiz
            acc_z = acc_z + mu_new * vert
            lam_old, mu_old, lam, mu = lam, mu, lam_new, mu_new
        adj_out.append(jnp.stack([lam, mu]))
        terms = jnp.stack([stretch * acc_h + couple * acc_x + acc_z, speed * acc_h, speed * acc_x])
        grad_total = grad_total + terms
    return grad_total, jnp.stack(fwd_out), jnp.stack(adj_out)
```

```python
import functools

import jax
import jax.numpy as jnp
from jax import lax
from jax.experimental import pallas as pl
from jax.experimental.pallas import tpu as pltpu
from jax.sharding import PartitionSpec as P

MESH = pl.DeviceIdType.MESH
F32 = jnp.float32
AZ, AX, AY, STEPS, NREC = 16, 128, 128, 6, 128
PAD = 8
GROUPS, DEEP = 4, 4


def kernel(
    n_shot,
    n_tile,
    coefs,
    fwd_state,
    adj_state,
    src_cell,
    src_wave,
    rec_cells,
    rec_row,
    observed_in,
    gradient,
    fwd_final,
    adj_final,
    cf,
    pp,
    qq,
    hs,
    zs,
    ll,
    mm,
    ff,
    oo,
    acc,
    rb,
    ry,
    hb,
    sb,
    picks,
    gath,
    spread,
    inj,
    observed,
    load_sem,
    out_sem,
    halo_send,
    halo_recv,
    whole_send,
    whole_recv,
    ag_send,
    ag_recv,
    rs_send,
    rs_recv,
):
    shot = lax.axis_index("shot")
    tile = lax.axis_index("tile")
    chip = shot // 2
    core = shot % 2
    sibling = chip * 2 + (1 - core)
    up = (shot + 2) % n_shot
    down = (shot + n_shot - 2) % n_shot
    left = (tile + n_tile - 1) % n_tile
    right = (tile + 1) % n_tile
    has_left = tile > 0
    has_right = tile < n_tile - 1
    mine = 2 * shot
    mine_sib = 2 * sibling
    above = (mine + 4) % AZ
    below = (mine + 12) % AZ
    far = (mine + 8) % AZ
    above_sib = (mine_sib + 4) % AZ
    below_sib = (mine_sib + 12) % AZ
    far_sib = (mine_sib + 8) % AZ

    own_load = pltpu.make_async_copy(coefs, cf.at[:, pl.ds(mine, 2)], load_sem.at[0])
    own_load.start()
    observed_load = pltpu.make_async_copy(observed_in, observed, load_sem.at[9])
    observed_load.start()
    body = pl.ds(PAD, AX)
    loads = []
    for i, (src, dst) in enumerate(
        (
            (fwd_state.at[0, 0], pp.at[0:AZ, body]),
            (fwd_state.at[0, 1], qq.at[2 : AZ + 2]),
            (fwd_state.at[0, 2], pp.at[AZ : 2 * AZ, body]),
            (fwd_state.at[0, 3], qq.at[AZ + 6 : 2 * AZ + 6]),
            (adj_state.at[0, 0], ll.at[0:AZ]),
            (adj_state.at[0, 1], mm.at[0:AZ]),
            (adj_state.at[0, 2], ll.at[AZ : 2 * AZ]),
            (adj_state.at[0, 3], mm.at[AZ : 2 * AZ]),
        )
    ):
        loads.append(pltpu.make_async_copy(src, dst, load_sem.at[1 + i]))

    def clear(i, carry):
        hb[pl.ds(i * 32, 32)] = jnp.zeros((32, AY), F32)
        return carry

    lax.fori_loop(0, 12, clear, 0)

    barrier = pltpu.get_barrier_semaphore()
    for other in (sibling, up, down):
        pl.semaphore_signal(barrier, inc=1, device_id=(other, tile), device_id_type=MESH)

    @pl.when(has_left)
    def _():
        pl.semaphore_signal(barrier, inc=1, device_id=(shot, left), device_id_type=MESH)

    @pl.when(has_right)
    def _():
        pl.semaphore_signal(barrier, inc=1, device_id=(shot, right), device_id_type=MESH)

    for copy in loads:
        copy.start()
    own_load.wait()
    cf[0, pl.ds(mine, 2)] = cf[0, pl.ds(mine, 2)] * F32(1.0 / 12.0)

    pl.semaphore_wait(barrier, 3 + jnp.minimum(tile, 1) + jnp.minimum(n_tile - 1 - tile, 1))

    def ag(index, layer, count, target):
        part = cf.at[:, pl.ds(layer, count)]
        return pltpu.make_async_remote_copy(
            src_ref=part,
            dst_ref=part,
            send_sem=ag_send.at[index],
            recv_sem=ag_recv.at[index],
            device_id=(target, tile),
            device_id_type=MESH,
        )

    send_up0 = ag(1, mine, 1, up)
    send_up1 = ag(2, mine + 1, 1, up)
    send_down0 = ag(3, mine + 1, 1, down)
    send_down1 = ag(4, mine, 1, down)
    send_sib = ag(0, mine, 2, sibling)
    for copy in (send_up0, send_down0, send_up1, send_down1, send_sib):
        copy.start()
    got_up0 = ag(1, below, 1, up)
    got_up1 = ag(2, below + 1, 1, up)
    got_down0 = ag(3, above + 1, 1, down)
    got_down1 = ag(4, above, 1, down)
    hop_up = ag(5, below, 1, up)
    hop_down = ag(6, above + 1, 1, down)
    got_hop_up = ag(5, far, 1, up)
    got_hop_down = ag(6, far + 1, 1, down)
    got_sib = ag(0, mine_sib, 2, sibling)
    pass_up0 = ag(7, below, 1, sibling)
    pass_down0 = ag(8, above + 1, 1, sibling)
    pass_up1 = ag(9, below + 1, 1, sibling)
    pass_down1 = ag(10, above, 1, sibling)
    pass_far0 = ag(11, far, 1, sibling)
    pass_far1 = ag(12, far + 1, 1, sibling)
    via_up0 = ag(7, below_sib, 1, sibling)
    via_down0 = ag(8, above_sib + 1, 1, sibling)
    via_up1 = ag(9, below_sib + 1, 1, sibling)
    via_down1 = ag(10, above_sib, 1, sibling)
    via_far0 = ag(11, far_sib, 1, sibling)
    via_far1 = ag(12, far_sib + 1, 1, sibling)

    none = jnp.zeros((AX, AY), F32)
    for base in (0, AZ + 4):
        for extra in (0, 1, AZ + 2, AZ + 3):
            qq[base + extra] = none
            oo[base + extra] = none

    marked = rec_row[...] >> 7
    gap = lax.broadcasted_iota(jnp.int32, (AY, AY), 0) - lax.broadcasted_iota(jnp.int32, (AY, AY), 1)
    gap = gap * gap
    taps = jnp.where(gap == 0, F32(-60), F32(0)) + jnp.where(gap == 1, F32(16), F32(0)) - jnp.where(gap == 4, F32(1), F32(0))
    taps = taps.astype(jnp.bfloat16)
    spread[2 * NREC : 3 * NREC] = taps
    spread[3 * NREC : 4 * NREC] = taps

    def mark(i, carry):
        rows = lax.broadcasted_iota(jnp.int32, (16, NREC), 0) + i * 16
        hit = jnp.where(rows == marked, F32(1.0), F32(0.0)).astype(jnp.bfloat16)
        at = pl.ds(pl.multiple_of(i * 16, 16), 16)
        picks[at, 0:NREC] = hit
        picks[at, NREC : 2 * NREC] = hit
        return carry

    lax.fori_loop(0, AZ * AX // 16, mark, 0)

    def halo(slot, group, to_right):
        src = sb.at[pl.ds((1 if to_right else 0) * 192 + slot * 32 + group * 8, 8)]
        dst = hb.at[pl.ds((0 if to_right else 1) * 192 + slot * 32 + group * 8, 8)]
        side = 0 if to_right else 1
        return pltpu.make_async_remote_copy(
            src_ref=src,
            dst_ref=dst,
            send_sem=halo_send.at[side, slot, group],
            recv_sem=halo_recv.at[side, slot, group],
            device_id=(shot, right if to_right else left),
            device_id_type=MESH,
        )

    def whole(slot, index, to_right):
        src = sb.at[pl.ds((1 if to_right else 0) * 192 + slot * 32, 32)]
        dst = hb.at[pl.ds((0 if to_right else 1) * 192 + slot * 32, 32)]
        side = 0 if to_right else 1
        return pltpu.make_async_remote_copy(
            src_ref=src,
            dst_ref=dst,
            send_sem=whole_send.at[side, index],
            recv_sem=whole_recv.at[side, index],
            device_id=(shot, right if to_right else left),
            device_id_type=MESH,
        )

    def both(build, act_left, act_right):
        @pl.when(has_left)
        def _():
            act_left(build)

        @pl.when(has_right)
        def _():
            act_right(build)

    def start(build):
        both(build, lambda b: b(False).start(), lambda b: b(True).start())

    def wait_send(build):
        both(build, lambda b: b(False).wait_send(), lambda b: b(True).wait_send())

    def wait_recv(build):
        both(build, lambda b: b(True).wait_recv(), lambda b: b(False).wait_recv())

    def stage_rows(field, at, slot, layer):
        sb[pl.ds(slot * 32 + layer * 2, 2)] = field[at, PAD : PAD + 2]
        sb[pl.ds(192 + slot * 32 + layer * 2, 2)] = field[at, PAD + AX - 2 : PAD + AX]

    def land_rows(field, at, slot, layer):
        field[at, PAD - 2 : PAD] = hb[pl.ds(slot * 32 + layer * 2, 2)]
        field[at, PAD + AX : PAD + AX + 2] = hb[pl.ds(192 + slot * 32 + layer * 2, 2)]

    loads[0].wait()

    def stage_first(d, carry):
        stage_rows(pp, d, 3, d)
        return carry

    lax.fori_loop(0, AZ, stage_first, 0)
    start(functools.partial(whole, 3, 0))

    lane = lax.broadcasted_iota(jnp.int32, (8, AY), 1)
    flat = lax.broadcasted_iota(jnp.int32, (8, AY), 0) * AY + lane

    def lap(field, at, r):
        def rows(k):
            return field[at, r + k : r + k + 8]

        one = rows(-1) + rows(1)
        two = rows(-2) + rows(2)
        return F32(16) * one - two

    def flat_terms(field, at, d):
        value = field[at, PAD : PAD + AX]
        high = value.astype(jnp.bfloat16)
        low = (value - high.astype(F32)).astype(jnp.bfloat16)
        if d is None:
            left_side = jnp.concatenate([high, low], axis=1)
            inj[...] = jnp.dot(left_side, spread[2 * NREC : 4 * NREC], preferred_element_type=F32)
        else:
            hits = picks[pl.ds(pl.multiple_of(d * AX, AX), AX)]
            left_side = jnp.concatenate([hits, high, low], axis=1)
            inj[...] = jnp.dot(left_side, spread[...], preferred_element_type=F32)

    def deep(field, at, r):
        def layer(k):
            return field[at + k, r : r + 8]

        return F32(16) * (layer(1) + layer(3)) - (layer(0) + layer(4)) - F32(30) * layer(2)

    def unrolled(fn):
        for t in range(AX // 8):
            fn(t)

    source = src_cell[0, 0]

    def gather_row(slot, parity, r, at_obs):
        cell = rec_cells[0, r]
        col = cell & (AY - 1)
        line = pp[parity * AZ + (cell >> 14), pl.ds(PAD + ((cell >> 7) & (AX - 1)), 1)]
        line = line - observed[0, at_obs, r]
        gath[slot, pl.ds(r, 1)] = jnp.where(lane[0:1] == col, line, F32(0))

    def forward_layer(n, cur, d, slot, order):
        nxt = 1 - cur
        here = cur * AZ + d
        there = nxt * AZ + d
        q_here = cur * (AZ + 4) + d
        q_there = nxt * (AZ + 4) + d + 2
        land_rows(pp, here, slot, d)
        wave = src_wave[0, n]
        start_cell = source - d * (AX * AY)
        obs_at = jnp.maximum(n - 1, 0)
        for j in range(8):
            gather_row(n, cur, order * 8 + j, obs_at)

        flat_terms(pp, here, None)

        def one(t):
            r = PAD + 8 * t
            c = cf[0, d, 8 * t : 8 * t + 8]
            a = cf[1, d, 8 * t : 8 * t + 8]
            b = cf[2, d, 8 * t : 8 * t + 8]
            h = lap(pp, here, r) + inj[8 * t : 8 * t + 8]
            z = deep(qq, q_here, 8 * t)
            hs[n * AZ + d, 8 * t : 8 * t + 8] = h
            zs[n * AZ + d, 8 * t : 8 * t + 8] = z
            pulse = jnp.where(flat == start_cell - 1024 * t, wave, F32(0))
            p = pp[here, r : r + 8]
            q = qq[q_here + 2, 8 * t : 8 * t + 8]
            p_new = (p + p) - pp[there, r : r + 8] + c * (a * h + b * z) + pulse
            q_new = (q + q) - qq[q_there, 8 * t : 8 * t + 8] + c * (b * h + z) + pulse
            pp[there, r : r + 8] = p_new
            qq[q_there, 8 * t : 8 * t + 8] = q_new

        unrolled(one)

    def scaled_layer(parity, d):
        def one(t):
            r = PAD + 8 * t
            at = pl.ds(8 * t, 8)
            c = cf[0, d, at]
            a = cf[1, d, at]
            b = cf[2, d, at]
            lam = ll[parity * AZ + d, at]
            mu = mm[parity * AZ + d, at]
            ff[parity * AZ + d, r : r + 8] = c * (a * lam + b * mu)
            oo[parity * (AZ + 4) + d + 2, at] = c * (b * lam + mu)

        unrolled(one)

    def ring_place(i):
        return (chip + i + i // 2 - 2 * (i // 3)) % GROUPS

    observed_load.wait()

    for i in range(1, 8):
        loads[i].wait()
    wait_recv(functools.partial(whole, 3, 0))
    got_sib.wait_recv()
    for i in range(GROUPS):
        if i == 1:
            got_up0.wait_recv()
            hop_up.start()
            pass_up0.start()
            got_down0.wait_recv()
            hop_down.start()
            pass_down0.start()
            got_up1.wait_recv()
            pass_up1.start()
            got_down1.wait_recv()
            pass_down1.start()
            via_down0.wait_recv()
            via_down1.wait_recv()
        if i == 2:
            via_up0.wait_recv()
            via_up1.wait_recv()
        if i == 3:
            got_hop_up.wait_recv()
            pass_far0.start()
            got_hop_down.wait_recv()
            pass_far1.start()
            via_far0.wait_recv()
            via_far1.wait_recv()
        group = ring_place(i)

        def layer0(j, carry, group=group, i=i):
            d = group * DEEP + j
            forward_layer(0, 0, d, 3, i * DEEP + j)
            stage_rows(pp, AZ + d, 1, d)
            scaled_layer(0, d)
            stage_rows(ff, d, 2, d)
            return carry

        lax.fori_loop(0, DEEP, layer0, 0)
        start(functools.partial(halo, 1, group))
    start(functools.partial(whole, 2, 1))

    def forward_step(n, carry):
        cur = n % 2

        def one_group(i, carry):
            group = ring_place(i)
            wait_recv(functools.partial(halo, cur, group))
            wait_send(functools.partial(halo, cur, group))

            def one_layer(j, carry):
                d = group * DEEP + j
                forward_layer(n, cur, d, cur, i * DEEP + j)
                stage_rows(pp, (1 - cur) * AZ + d, 1 - cur, d)
                return carry

            lax.fori_loop(0, DEEP, one_layer, 0)

            @pl.when(n < STEPS - 1)
            def _():
                start(functools.partial(halo, 1 - cur, group))

            return carry

        lax.fori_loop(0, GROUPS, one_group, 0)
        return carry

    lax.fori_loop(1, STEPS, forward_step, 0)

    out_p = pltpu.make_async_copy(pp.at[0:AZ, body], fwd_final.at[0, 0], out_sem.at[0])
    out_q = pltpu.make_async_copy(qq.at[2 : AZ + 2], fwd_final.at[0, 1], out_sem.at[1])
    out_p.start()
    out_q.start()

    def gather_last(i, carry):
        for j in range(8):
            gather_row(STEPS, 0, i * 8 + j, STEPS - 1)
        return carry

    lax.fori_loop(0, NREC // 8, gather_last, 0)

    def adj_layer(s, cur, d, slot, mode):
        nxt = 1 - cur
        here = cur * AZ + d
        there = nxt * AZ + d
        o_here = cur * (AZ + 4) + d
        o_there = nxt * (AZ + 4) + d + 2
        k = STEPS - s
        land_rows(ff, here, slot, d)
        flat_terms(ff, here, d)

        def one(t):
            r = PAD + 8 * t
            at = pl.ds(8 * t, 8)
            lam = ll[here, at]
            mu = mm[here, at]
            lam_old = ll[there, at]
            mu_old = mm[there, at]
            lam_new = inj[at] + (lam + lam) - lam_old + lap(ff, here, r)
            mu_new = (mu + mu) - mu_old + deep(oo, o_here, 8 * t)
            ll[there, at] = lam_new
            mm[there, at] = mu_new
            if mode != "last":
                c = cf[0, d, at]
                a = cf[1, d, at]
                b = cf[2, d, at]
                ff[there, r : r + 8] = c * (a * lam_new + b * mu_new)
                oo[o_there, at] = c * (b * lam_new + mu_new)
            if mode != "plain":
                h0 = hs[(k - 1) * AZ + d, at]
                z0 = zs[(k - 1) * AZ + d, at]
                h1 = hs[k * AZ + d, at]
                z1 = zs[k * AZ + d, at]
                h2 = hs[(k + 1) * AZ + d, at]
                z2 = zs[(k + 1) * AZ + d, at]
                q_h = lam_new * h0 + lam * h1 + lam_old * h2
                q_x = (lam_new * z0 + mu_new * h0) + (lam * z1 + mu * h1) + (lam_old * z2 + mu_old * h2)
                q_z = mu_new * z0 + mu * z1 + mu_old * z2
                if mode == "last":
                    q_h += acc[0, d, at]
                    q_x += acc[1, d, at]
                    q_z += acc[2, d, at]
                acc[0, d, at] = q_h
                acc[1, d, at] = q_x
                acc[2, d, at] = q_z

        unrolled(one)

    def set_spread(k):
        value = gath[k]
        high = value.astype(jnp.bfloat16)
        spread[0:NREC] = high
        spread[NREC : 2 * NREC] = (value - high.astype(F32)).astype(jnp.bfloat16)

    def adj_step(s, first, mode, carry):
        cur = s % 2
        slot = 2 if first else 4 + cur
        set_spread(STEPS - s)

        def one_group(i, carry):
            group = ring_place(i)
            if not first:
                wait_recv(functools.partial(halo, slot, group))
                wait_send(functools.partial(halo, slot, group))

            def one_layer(j, carry):
                d = group * DEEP + j
                adj_layer(s, cur, d, slot, mode)
                stage_rows(ff, (1 - cur) * AZ + d, 5 - cur, d)
                return carry

            lax.fori_loop(0, DEEP, one_layer, 0)
            start(functools.partial(halo, 5 - cur, group))
            return carry

        lax.fori_loop(0, GROUPS, one_group, 0)
        return carry

    wait_recv(functools.partial(whole, 2, 1))
    adj_step(0, True, "plain", 0)
    adj_step(1, False, "plain", 0)
    adj_step(2, False, "third", 0)
    lax.fori_loop(3, 5, lambda s, carry: adj_step(s, False, "plain", carry), 0)

    def exchange(i, group):
        layer = group * DEEP
        return pltpu.make_async_remote_copy(
            src_ref=acc.at[:, pl.ds(layer + 2 * (1 - core), 2)],
            dst_ref=rb.at[:, pl.ds(2 * i, 2)],
            send_sem=rs_send.at[i],
            recv_sem=rs_recv.at[i],
            device_id=(sibling, tile),
            device_id_type=MESH,
        )

    def ring(index, layer, target):
        return pltpu.make_async_remote_copy(
            src_ref=acc.at[:, pl.ds(layer, 1)],
            dst_ref=ry.at[:, pl.ds(index, 1)],
            send_sem=rs_send.at[4 + index],
            recv_sem=rs_recv.at[4 + index],
            device_id=(target, tile),
            device_id_type=MESH,
        )

    def add_pair(i, group):
        layer = group * DEEP + 2 * core

        def add(t, carry):
            at = pl.ds(pl.multiple_of(t * 16, 16), 16)
            for f in range(3):
                for e in range(2):
                    acc[f, layer + e, at] = acc[f, layer + e, at] + rb[f, 2 * i + e, at]
            return carry

        lax.fori_loop(0, AX // 16, add, 0)

    def add_hop(index, layer):
        def add(t, carry):
            at = pl.ds(pl.multiple_of(t * 16, 16), 16)
            for f in range(3):
                acc[f, layer, at] = acc[f, layer, at] + ry[f, index, at]
            return carry

        lax.fori_loop(0, AX // 16, add, 0)

    to_up0 = ring(0, far, up)
    to_down0 = ring(1, far + 1, down)
    to_up1 = ring(2, above + 1, up)
    to_down1 = ring(3, below, down)
    to_up2 = ring(4, above, up)
    to_down2 = ring(5, below + 1, down)

    set_spread(1)
    groups = [(chip + k) % GROUPS for k in (2, 3, 1, 0)]
    swaps = [exchange(i, groups[i]) for i in range(GROUPS)]

    def summed(i):
        swaps[i].wait_send()
        swaps[i].wait_recv()
        add_pair(i, groups[i])
        if i == 0:
            to_up0.start()
            to_down0.start()
        if i == 1:
            to_down1.start()
        if i == 2:
            to_up1.start()

    for i in range(GROUPS):
        group = groups[i]
        wait_recv(functools.partial(halo, 5, group))
        wait_send(functools.partial(halo, 5, group))

        def last_layer(j, carry, group=group):
            adj_layer(5, 1, group * DEEP + j, 5, "last")
            return carry

        lax.fori_loop(0, DEEP, last_layer, 0)
        swaps[i].start()
        if i > 0:
            summed(i - 1)
    out_l = pltpu.make_async_copy(ll.at[0:AZ], adj_final.at[0, 0], out_sem.at[2])
    out_m = pltpu.make_async_copy(mm.at[0:AZ], adj_final.at[0, 1], out_sem.at[3])
    out_l.start()
    out_m.start()
    summed(GROUPS - 1)
    to_up0.wait_recv()
    add_hop(0, above)
    to_up2.start()
    to_down0.wait_recv()
    add_hop(1, below + 1)
    to_down2.start()
    to_up1.wait_recv()
    to_down1.wait_recv()
    to_up2.wait_recv()
    to_down2.wait_recv()

    def finish(t, carry):
        at = pl.ds(pl.multiple_of(t * 16, 16), 16)
        for e, (direct, passed) in enumerate(((3, 4), (2, 5))):
            q_h, q_x, q_z = (
                acc[f, mine + e, at] + ry[f, direct, at] + ry[f, passed, at] for f in range(3)
            )
            c = cf[0, mine + e, at]
            a = cf[1, mine + e, at]
            b = cf[2, mine + e, at]
            gradient[0, e, at] = (a * q_h + b * q_x + q_z) * F32(1.0 / 12.0)
            gradient[1, e, at] = c * q_h
            gradient[2, e, at] = c * q_x
        return carry

    lax.fori_loop(0, AX // 16, finish, 0)

    for copy in (send_up0, send_down0, send_up1, send_down1, send_sib, hop_up, hop_down):
        copy.wait_send()
    for copy in (pass_up0, pass_down0, pass_up1, pass_down1, pass_far0, pass_far1):
        copy.wait_send()
    for copy in (to_up0, to_down0, to_up1, to_down1, to_up2, to_down2):
        copy.wait_send()
    wait_send(functools.partial(whole, 3, 0))
    wait_send(functools.partial(whole, 2, 1))
    out_p.wait()
    out_q.wait()
    out_l.wait()
    out_m.wait()


def solution(mesh):
    n_shot, n_tile = mesh.shape["shot"], mesh.shape["tile"]

    def per_device(coefs, fwd_state, adj_state, src_cell, src_wave, rec_cells, observed):
        hbm = pl.BlockSpec(memory_space=pl.ANY)
        smem = pl.BlockSpec(memory_space=pltpu.SMEM)
        vmem = pl.BlockSpec(memory_space=pltpu.VMEM)
        dma = pltpu.SemaphoreType.DMA
        return pl.pallas_call(
            functools.partial(kernel, n_shot, n_tile),
            out_shape=(
                jax.ShapeDtypeStruct((3, 2, AX, AY), F32),
                jax.ShapeDtypeStruct((1, 2, AZ, AX, AY), F32),
                jax.ShapeDtypeStruct((1, 2, AZ, AX, AY), F32),
            ),
            in_specs=[hbm, hbm, hbm, smem, smem, smem, vmem, hbm],
            out_specs=(vmem, hbm, hbm),
            scratch_shapes=[
                pltpu.VMEM((3, AZ, AX, AY), F32),
                pltpu.VMEM((2 * AZ, AX + 2 * PAD, AY), F32),
                pltpu.VMEM((2 * (AZ + 4), AX, AY), F32),
                pltpu.VMEM((STEPS * AZ, AX, AY), F32),
                pltpu.VMEM((STEPS * AZ, AX, AY), F32),
                pltpu.VMEM((2 * AZ, AX, AY), F32),
                pltpu.VMEM((2 * AZ, AX, AY), F32),
                pltpu.VMEM((2 * AZ, AX + 2 * PAD, AY), F32),
                pltpu.VMEM((2 * (AZ + 4), AX, AY), F32),
                pltpu.VMEM((3, AZ, AX, AY), F32),
                pltpu.VMEM((3, 8, AX, AY), F32),
                pltpu.VMEM((3, 6, AX, AY), F32),
                pltpu.VMEM((2 * 192, AY), F32),
                pltpu.VMEM((2 * 192, AY), F32),
                pltpu.VMEM((AZ * AX, 2 * NREC), jnp.bfloat16),
                pltpu.VMEM((STEPS + 1, NREC, AY), F32),
                pltpu.VMEM((4 * NREC, AY), jnp.bfloat16),
                pltpu.VMEM((AX, AY), F32),
                pltpu.SMEM((1, STEPS, NREC), F32),
                dma((10,)),
                dma((4,)),
                dma((2, 6, 4)),
                dma((2, 6, 4)),
                dma((2, 2)),
                dma((2, 2)),
                dma((13,)),
                dma((13,)),
                dma((10,)),
                dma((10,)),
            ],
            compiler_params=pltpu.CompilerParams(
                collective_id=0, has_side_effects=True, vmem_limit_bytes=56 * 1024 * 1024
            ),
        )(coefs, fwd_state, adj_state, src_cell, src_wave, rec_cells, rec_cells, observed)

    placed = (
        P(None, "shot", "tile", None),
        P("shot", None, None, "tile", None),
        P("shot", None, None, "tile", None),
        P("shot", "tile"),
        P("shot", None),
        P("shot", "tile"),
        P("shot", None, "tile"),
    )
    return jax.shard_map(
        per_device,
        mesh=mesh,
        in_specs=placed,
        out_specs=(
            P(None, "shot", "tile", None),
            P("shot", None, None, "tile", None),
            P("shot", None, None, "tile", None),
        ),
        check_vma=False,
    )
```

```python
import functools

import jax
import jax.numpy as jnp
from jax import lax
from jax.experimental import pallas as pl
from jax.experimental.pallas import tpu as pltpu
from jax.sharding import PartitionSpec as P

MESH = pl.DeviceIdType.MESH
F32 = jnp.float32
AZ, AX, AY, STEPS, NREC = 16, 128, 128, 6, 128
PAD = 8
GROUPS, DEEP = 4, 4


def kernel(
    n_shot,
    n_tile,
    coefs,
    fwd_state,
    adj_state,
    src_cell,
    src_wave,
    rec_cells,
    rec_row,
    observed_in,
    gradient,
    fwd_final,
    adj_final,
    cf,
    pp,
    qq,
    hs,
    zs,
    ll,
    mm,
    ff,
    oo,
    acc,
    rb,
    ry,
    hb,
    sb,
    picks,
    gath,
    spread,
    terms_a,
    terms_b,
    observed,
    load_sem,
    out_sem,
    halo_send,
    halo_recv,
    whole_send,
    whole_recv,
    ag_send,
    ag_recv,
    rs_send,
    rs_recv,
):
    shot = lax.axis_index("shot")
    tile = lax.axis_index("tile")
    chip = shot // 2
    core = shot % 2
    sibling = chip * 2 + (1 - core)
    up = (shot + 2) % n_shot
    down = (shot + n_shot - 2) % n_shot
    left = (tile + n_tile - 1) % n_tile
    right = (tile + 1) % n_tile
    has_left = tile > 0
    has_right = tile < n_tile - 1
    mine = 2 * shot
    mine_sib = 2 * sibling
    above = (mine + 4) % AZ
    below = (mine + 12) % AZ
    far = (mine + 8) % AZ
    above_sib = (mine_sib + 4) % AZ
    below_sib = (mine_sib + 12) % AZ
    far_sib = (mine_sib + 8) % AZ

    own_load = pltpu.make_async_copy(coefs, cf.at[:, pl.ds(mine, 2)], load_sem.at[0])
    own_load.start()
    observed_load = pltpu.make_async_copy(observed_in, observed, load_sem.at[9])
    observed_load.start()
    body = pl.ds(PAD, AX)
    loads = []
    for i, (src, dst) in enumerate(
        (
            (fwd_state.at[0, 0], pp.at[0:AZ, body]),
            (fwd_state.at[0, 1], qq.at[2 : AZ + 2]),
            (fwd_state.at[0, 2], pp.at[AZ : 2 * AZ, body]),
            (fwd_state.at[0, 3], qq.at[AZ + 6 : 2 * AZ + 6]),
            (adj_state.at[0, 0], ll.at[0:AZ]),
            (adj_state.at[0, 1], mm.at[0:AZ]),
            (adj_state.at[0, 2], ll.at[AZ : 2 * AZ]),
            (adj_state.at[0, 3], mm.at[AZ : 2 * AZ]),
        )
    ):
        loads.append(pltpu.make_async_copy(src, dst, load_sem.at[1 + i]))

    def clear(i, carry):
        hb[pl.ds(i * 32, 32)] = jnp.zeros((32, AY), F32)
        return carry

    lax.fori_loop(0, 12, clear, 0)

    barrier = pltpu.get_barrier_semaphore()
    for other in (sibling, up, down):
        pl.semaphore_signal(barrier, inc=1, device_id=(other, tile), device_id_type=MESH)

    @pl.when(has_left)
    def _():
        pl.semaphore_signal(barrier, inc=1, device_id=(shot, left), device_id_type=MESH)

    @pl.when(has_right)
    def _():
        pl.semaphore_signal(barrier, inc=1, device_id=(shot, right), device_id_type=MESH)

    for copy in loads:
        copy.start()
    own_load.wait()
    cf[0, pl.ds(mine, 2)] = cf[0, pl.ds(mine, 2)] * F32(1.0 / 12.0)

    pl.semaphore_wait(barrier, 3 + jnp.minimum(tile, 1) + jnp.minimum(n_tile - 1 - tile, 1))

    def ag(index, layer, count, target):
        part = cf.at[:, pl.ds(layer, count)]
        return pltpu.make_async_remote_copy(
            src_ref=part,
            dst_ref=part,
            send_sem=ag_send.at[index],
            recv_sem=ag_recv.at[index],
            device_id=(target, tile),
            device_id_type=MESH,
        )

    send_up0 = ag(1, mine, 1, up)
    send_up1 = ag(2, mine + 1, 1, up)
    send_down0 = ag(3, mine + 1, 1, down)
    send_down1 = ag(4, mine, 1, down)
    send_sib = ag(0, mine, 2, sibling)
    for copy in (send_up0, send_down0, send_up1, send_down1, send_sib):
        copy.start()
    got_up0 = ag(1, below, 1, up)
    got_up1 = ag(2, below + 1, 1, up)
    got_down0 = ag(3, above + 1, 1, down)
    got_down1 = ag(4, above, 1, down)
    hop_up = ag(5, below, 1, up)
    hop_down = ag(6, above + 1, 1, down)
    got_hop_up = ag(5, far, 1, up)
    got_hop_down = ag(6, far + 1, 1, down)
    got_sib = ag(0, mine_sib, 2, sibling)
    pass_up0 = ag(7, below, 1, sibling)
    pass_down0 = ag(8, above + 1, 1, sibling)
    pass_up1 = ag(9, below + 1, 1, sibling)
    pass_down1 = ag(10, above, 1, sibling)
    pass_far0 = ag(11, far, 1, sibling)
    pass_far1 = ag(12, far + 1, 1, sibling)
    via_up0 = ag(7, below_sib, 1, sibling)
    via_down0 = ag(8, above_sib + 1, 1, sibling)
    via_up1 = ag(9, below_sib + 1, 1, sibling)
    via_down1 = ag(10, above_sib, 1, sibling)
    via_far0 = ag(11, far_sib, 1, sibling)
    via_far1 = ag(12, far_sib + 1, 1, sibling)

    none = jnp.zeros((AX, AY), F32)
    for base in (0, AZ + 4):
        for extra in (0, 1, AZ + 2, AZ + 3):
            qq[base + extra] = none
            oo[base + extra] = none

    marked = rec_row[...] >> 7
    gap = lax.broadcasted_iota(jnp.int32, (AY, AY), 0) - lax.broadcasted_iota(jnp.int32, (AY, AY), 1)
    gap = gap * gap
    taps = jnp.where(gap == 0, F32(-60), F32(0)) + jnp.where(gap == 1, F32(16), F32(0)) - jnp.where(gap == 4, F32(1), F32(0))
    taps = taps.astype(jnp.bfloat16)
    for k in (2, 3, 6, 7):
        spread[k * NREC : (k + 1) * NREC] = taps

    def mark(i, carry):
        rows = lax.broadcasted_iota(jnp.int32, (16, NREC), 0) + i * 16
        hit = jnp.where(rows == marked, F32(1.0), F32(0.0)).astype(jnp.bfloat16)
        at = pl.ds(pl.multiple_of(i * 16, 16), 16)
        picks[at, 0:NREC] = hit
        picks[at, NREC : 2 * NREC] = hit
        return carry

    lax.fori_loop(0, AZ * AX // 16, mark, 0)

    def halo(slot, group, to_right):
        src = sb.at[pl.ds((1 if to_right else 0) * 192 + slot * 32 + group * 8, 8)]
        dst = hb.at[pl.ds((0 if to_right else 1) * 192 + slot * 32 + group * 8, 8)]
        side = 0 if to_right else 1
        return pltpu.make_async_remote_copy(
            src_ref=src,
            dst_ref=dst,
            send_sem=halo_send.at[side, slot, group],
            recv_sem=halo_recv.at[side, slot, group],
            device_id=(shot, right if to_right else left),
            device_id_type=MESH,
        )

    def whole(slot, index, to_right):
        src = sb.at[pl.ds((1 if to_right else 0) * 192 + slot * 32, 32)]
        dst = hb.at[pl.ds((0 if to_right else 1) * 192 + slot * 32, 32)]
        side = 0 if to_right else 1
        return pltpu.make_async_remote_copy(
            src_ref=src,
            dst_ref=dst,
            send_sem=whole_send.at[side, index],
            recv_sem=whole_recv.at[side, index],
            device_id=(shot, right if to_right else left),
            device_id_type=MESH,
        )

    def both(build, act_left, act_right):
        @pl.when(has_left)
        def _():
            act_left(build)

        @pl.when(has_right)
        def _():
            act_right(build)

    def start(build):
        both(build, lambda b: b(False).start(), lambda b: b(True).start())

    def wait_send(build):
        both(build, lambda b: b(False).wait_send(), lambda b: b(True).wait_send())

    def wait_recv(build):
        both(build, lambda b: b(True).wait_recv(), lambda b: b(False).wait_recv())

    def stage_rows(field, at, slot, layer):
        sb[pl.ds(slot * 32 + layer * 2, 2)] = field[at, PAD : PAD + 2]
        sb[pl.ds(192 + slot * 32 + layer * 2, 2)] = field[at, PAD + AX - 2 : PAD + AX]

    def land_rows(field, at, slot, layer):
        field[at, PAD - 2 : PAD] = hb[pl.ds(slot * 32 + layer * 2, 2)]
        field[at, PAD + AX : PAD + AX + 2] = hb[pl.ds(192 + slot * 32 + layer * 2, 2)]

    loads[0].wait()

    def stage_first(d, carry):
        stage_rows(pp, d, 3, d)
        return carry

    lax.fori_loop(0, AZ, stage_first, 0)
    start(functools.partial(whole, 3, 0))

    lane = lax.broadcasted_iota(jnp.int32, (1, AY), 1)
    flat = lax.broadcasted_iota(jnp.int32, (8, AY), 0) * AY + lax.broadcasted_iota(jnp.int32, (8, AY), 1)
    source = src_cell[0, 0]

    def ring_place(i):
        return (chip + i + i // 2 - 2 * (i // 3)) % GROUPS

    def lap(field, at, r):
        def rows(k):
            return field[at, r + k : r + k + 8]

        return F32(16) * (rows(-1) + rows(1)) - (rows(-2) + rows(2))

    def deep(layers):
        return F32(16) * (layers[1] + layers[3]) - (layers[0] + layers[4]) - F32(30) * layers[2]

    def flat_terms(field, parity, d, out, side):
        value = field[pl.ds(parity * AZ + d, 2), PAD : PAD + AX].reshape(2 * AX, AY)
        high = value.astype(jnp.bfloat16)
        low = (value - high.astype(F32)).astype(jnp.bfloat16)
        if side is None:
            left_side = jnp.concatenate([high, low], axis=1)
            out[...] = jnp.dot(left_side, spread[2 * NREC : 4 * NREC], preferred_element_type=F32)
        else:
            hits = picks[pl.ds(pl.multiple_of(d * AX, AX), 2 * AX)]
            left_side = jnp.concatenate([hits, high, low], axis=1)
            right_side = spread[pl.ds(pl.multiple_of(side * 4 * NREC, 4 * NREC), 4 * NREC)]
            out[...] = jnp.dot(left_side, right_side, preferred_element_type=F32)

    def gather_row(slot, parity, r, at_obs):
        cell = rec_cells[0, r]
        col = cell & (AY - 1)
        line = pp[parity * AZ + (cell >> 14), pl.ds(PAD + ((cell >> 7) & (AX - 1)), 1)]
        line = line - observed[at_obs, 0, r]
        gath[slot, pl.ds(r, 1)] = jnp.where(lane == col, line, F32(0))

    def forward_pair(n, cur, d, terms):
        nxt = 1 - cur
        here = cur * AZ + d
        there = nxt * AZ + d
        q_here = cur * (AZ + 4) + d
        q_there = nxt * (AZ + 4) + d + 2
        wave = src_wave[0, n]
        start_cell = source - d * (AX * AY)
        for t in range(AX // 8):
            r = PAD + 8 * t
            at = slice(8 * t, 8 * t + 8)
            layers = [qq[q_here + k, at] for k in range(6)]
            for e in range(2):
                c = cf[0, d + e, at]
                a = cf[1, d + e, at]
                b = cf[2, d + e, at]
                h = lap(pp, here + e, r) + terms[e * AX + 8 * t : e * AX + 8 * t + 8]
                z = deep(layers[e : e + 5])
                hs[n * AZ + d + e, at] = h
                zs[n * AZ + d + e, at] = z
                pulse = jnp.where(flat == start_cell - (AX * AY * e + 1024 * t), wave, F32(0))
                p = pp[here + e, r : r + 8]
                q = layers[e + 2]
                pp[there + e, r : r + 8] = (p + p) - pp[there + e, r : r + 8] + c * (a * h + b * z) + pulse
                qq[q_there + e, at] = (q + q) - qq[q_there + e, at] + c * (b * h + z) + pulse

    def scaled_pair(d):
        for t in range(AX // 8):
            r = PAD + 8 * t
            at = slice(8 * t, 8 * t + 8)
            for e in range(2):
                c = cf[0, d + e, at]
                a = cf[1, d + e, at]
                b = cf[2, d + e, at]
                lam = ll[d + e, at]
                mu = mm[d + e, at]
                ff[d + e, r : r + 8] = c * (a * lam + b * mu)
                oo[d + e + 2, at] = c * (b * lam + mu)

    def forward_group(n, cur, i, group, slot):
        d = group * DEEP
        for e in range(DEEP):
            land_rows(pp, cur * AZ + d + e, slot, d + e)
        after = (cur + (i + 1) // GROUPS) % 2
        obs_at = jnp.maximum(n - 1, 0)
        flat_terms(pp, cur, d + 2, terms_b, None)
        for j in range(16):
            gather_row(n, cur, i * 32 + j, obs_at)
        forward_pair(n, cur, d, terms_a)
        flat_terms(pp, after, ring_place((i + 1) % GROUPS) * DEEP, terms_a, None)
        for j in range(16, 32):
            gather_row(n, cur, i * 32 + j, obs_at)
        forward_pair(n, cur, d + 2, terms_b)
        for e in range(DEEP):
            stage_rows(pp, (1 - cur) * AZ + d + e, 1 - cur, d + e)

    flat_terms(pp, 0, ring_place(0) * DEEP, terms_a, None)
    observed_load.wait()
    for i in range(1, 8):
        loads[i].wait()
    wait_recv(functools.partial(whole, 3, 0))
    got_sib.wait_recv()

    def first_group(i, carry):
        @pl.when(i == 1)
        def _():
            got_up0.wait_recv()
            hop_up.start()
            pass_up0.start()
            got_down0.wait_recv()
            hop_down.start()
            pass_down0.start()
            got_up1.wait_recv()
            pass_up1.start()
            got_down1.wait_recv()
            pass_down1.start()
            via_down0.wait_recv()
            via_down1.wait_recv()

        @pl.when(i == 2)
        def _():
            via_up0.wait_recv()
            via_up1.wait_recv()

        @pl.when(i == 3)
        def _():
            got_hop_up.wait_recv()
            pass_far0.start()
            got_hop_down.wait_recv()
            pass_far1.start()
            via_far0.wait_recv()
            via_far1.wait_recv()

        group = ring_place(i)
        d = group * DEEP
        forward_group(0, 0, i, group, 3)
        start(functools.partial(halo, 1, group))
        scaled_pair(d)
        scaled_pair(d + 2)
        for e in range(DEEP):
            stage_rows(ff, d + e, 4, d + e)
        start(functools.partial(halo, 4, group))
        return carry

    lax.fori_loop(0, GROUPS, first_group, 0)

    def forward_step(n, carry):
        cur = n % 2

        def one_group(i, carry):
            group = ring_place(i)
            wait_recv(functools.partial(halo, cur, group))
            wait_send(functools.partial(halo, cur, group))
            forward_group(n, cur, i, group, cur)

            @pl.when(n < STEPS - 1)
            def _():
                start(functools.partial(halo, 1 - cur, group))

            return carry

        lax.fori_loop(0, GROUPS, one_group, 0)
        return carry

    lax.fori_loop(1, STEPS, forward_step, 0)

    out_p = pltpu.make_async_copy(pp.at[0:AZ, body], fwd_final.at[0, 0], out_sem.at[0])
    out_q = pltpu.make_async_copy(qq.at[2 : AZ + 2], fwd_final.at[0, 1], out_sem.at[1])
    out_p.start()
    out_q.start()

    def gather_last(i, carry):
        for j in range(16):
            gather_row(STEPS, 0, i * 16 + j, STEPS - 1)
        return carry

    lax.fori_loop(0, NREC // 16, gather_last, 0)

    def adj_pair(s, cur, d, terms, mode):
        nxt = 1 - cur
        here = cur * AZ + d
        there = nxt * AZ + d
        o_here = cur * (AZ + 4) + d
        o_there = nxt * (AZ + 4) + d + 2
        k = STEPS - s
        for t in range(AX // 8):
            r = PAD + 8 * t
            at = slice(8 * t, 8 * t + 8)
            layers = [oo[o_here + n, at] for n in range(6)]
            for e in range(2):
                lam = ll[here + e, at]
                mu = mm[here + e, at]
                lam_old = ll[there + e, at]
                mu_old = mm[there + e, at]
                mix = terms[e * AX + 8 * t : e * AX + 8 * t + 8]
                lam_new = (lam + lam) - lam_old + lap(ff, here + e, r) + mix
                mu_new = (mu + mu) - mu_old + deep(layers[e : e + 5])
                ll[there + e, at] = lam_new
                mm[there + e, at] = mu_new
                if mode != "last":
                    c = cf[0, d + e, at]
                    a = cf[1, d + e, at]
                    b = cf[2, d + e, at]
                    ff[there + e, r : r + 8] = c * (a * lam_new + b * mu_new)
                    oo[o_there + e, at] = c * (b * lam_new + mu_new)
                if mode != "plain":
                    h0 = hs[(k - 1) * AZ + d + e, at]
                    z0 = zs[(k - 1) * AZ + d + e, at]
                    h1 = hs[k * AZ + d + e, at]
                    z1 = zs[k * AZ + d + e, at]
                    h2 = hs[(k + 1) * AZ + d + e, at]
                    z2 = zs[(k + 1) * AZ + d + e, at]
                    q_h = lam_new * h0 + lam * h1 + lam_old * h2
                    q_x = (lam_new * z0 + mu_new * h0) + (lam * z1 + mu * h1) + (lam_old * z2 + mu_old * h2)
                    q_z = mu_new * z0 + mu * z1 + mu_old * z2
                    if mode == "last":
                        q_h += acc[0, d + e, at]
                        q_x += acc[1, d + e, at]
                        q_z += acc[2, d + e, at]
                    acc[0, d + e, at] = q_h
                    acc[1, d + e, at] = q_x
                    acc[2, d + e, at] = q_z

    def set_spread(k, side):
        value = gath[k]
        high = value.astype(jnp.bfloat16)
        low = (value - high.astype(F32)).astype(jnp.bfloat16)
        base = pl.multiple_of(side * 4 * NREC, 4 * NREC)
        spread[pl.ds(base, 2 * NREC)] = jnp.concatenate([high, low], axis=0)

    def last_place(i):
        return (chip + 2 + i - 3 * (i // 2) - 2 * (i // 3)) % GROUPS

    def adj_group(s, cur, i, mode, place):
        group = place(i)
        d = group * DEEP
        slot = 4 + cur
        wait_recv(functools.partial(halo, slot, group))
        wait_send(functools.partial(halo, slot, group))
        for e in range(DEEP):
            land_rows(ff, cur * AZ + d + e, slot, d + e)
        flat_terms(ff, cur, d + 2, terms_b, cur)
        adj_pair(s, cur, d, terms_a, mode)
        flat_terms(ff, cur, place((i + 1) % GROUPS) * DEEP, terms_a, cur)
        adj_pair(s, cur, d + 2, terms_b, mode)
        if mode != "last":
            for e in range(DEEP):
                stage_rows(ff, (1 - cur) * AZ + d + e, 5 - cur, d + e)
            start(functools.partial(halo, 5 - cur, group))

    def adj_step(s, mode, carry):
        cur = s % 2
        set_spread(STEPS - s, cur)
        flat_terms(ff, cur, ring_place(0) * DEEP, terms_a, cur)

        def one_group(i, carry):
            adj_group(s, cur, i, mode, ring_place)
            return carry

        lax.fori_loop(0, GROUPS, one_group, 0)
        return carry

    lax.fori_loop(0, 2, lambda s, carry: adj_step(s, "plain", carry), 0)
    adj_step(2, "third", 0)
    lax.fori_loop(3, 5, lambda s, carry: adj_step(s, "plain", carry), 0)

    def exchange(i, group):
        layer = group * DEEP
        return pltpu.make_async_remote_copy(
            src_ref=acc.at[:, pl.ds(layer + 2 * (1 - core), 2)],
            dst_ref=rb.at[:, pl.ds(2 * i, 2)],
            send_sem=rs_send.at[i],
            recv_sem=rs_recv.at[i],
            device_id=(sibling, tile),
            device_id_type=MESH,
        )

    def ring(index, layer, target):
        return pltpu.make_async_remote_copy(
            src_ref=acc.at[:, pl.ds(layer, 1)],
            dst_ref=ry.at[:, pl.ds(index, 1)],
            send_sem=rs_send.at[4 + index],
            recv_sem=rs_recv.at[4 + index],
            device_id=(target, tile),
            device_id_type=MESH,
        )

    def add_pair(i, group):
        layer = group * DEEP + 2 * core

        def add(t, carry):
            at = pl.ds(pl.multiple_of(t * 16, 16), 16)
            for f in range(3):
                for e in range(2):
                    acc[f, layer + e, at] = acc[f, layer + e, at] + rb[f, 2 * i + e, at]
            return carry

        lax.fori_loop(0, AX // 16, add, 0)

    def add_hop(index, layer):
        def add(t, carry):
            at = pl.ds(pl.multiple_of(t * 16, 16), 16)
            for f in range(3):
                acc[f, layer, at] = acc[f, layer, at] + ry[f, index, at]
            return carry

        lax.fori_loop(0, AX // 16, add, 0)

    to_up0 = ring(0, far, up)
    to_down0 = ring(1, far + 1, down)
    to_up1 = ring(2, above + 1, up)
    to_down1 = ring(3, below, down)
    to_up2 = ring(4, above, up)
    to_down2 = ring(5, below + 1, down)

    set_spread(1, 1)
    flat_terms(ff, 1, last_place(0) * DEEP, terms_a, 1)

    def swap(i):
        return exchange(i, last_place(i))

    def summed(i):
        swap(i).wait_send()
        swap(i).wait_recv()
        add_pair(i, last_place(i))

    def last_group(i, carry):
        adj_group(5, 1, i, "last", last_place)
        swap(i).start()

        @pl.when(i > 0)
        def _():
            summed(i - 1)

        @pl.when(i == 1)
        def _():
            to_up0.start()
            to_down0.start()

        @pl.when(i == 2)
        def _():
            to_down1.start()

        @pl.when(i == 3)
        def _():
            to_up1.start()

        return carry

    lax.fori_loop(0, GROUPS, last_group, 0)
    out_l = pltpu.make_async_copy(ll.at[0:AZ], adj_final.at[0, 0], out_sem.at[2])
    out_m = pltpu.make_async_copy(mm.at[0:AZ], adj_final.at[0, 1], out_sem.at[3])
    out_l.start()
    out_m.start()
    summed(GROUPS - 1)
    to_up0.wait_recv()
    add_hop(0, above)
    to_up2.start()
    to_down0.wait_recv()
    add_hop(1, below + 1)
    to_down2.start()
    to_up1.wait_recv()
    to_down1.wait_recv()
    to_up2.wait_recv()
    to_down2.wait_recv()

    def finish(t, carry):
        at = pl.ds(pl.multiple_of(t * 16, 16), 16)
        for e, (direct, passed) in enumerate(((3, 4), (2, 5))):
            q_h, q_x, q_z = (
                acc[f, mine + e, at] + ry[f, direct, at] + ry[f, passed, at] for f in range(3)
            )
            c = cf[0, mine + e, at]
            a = cf[1, mine + e, at]
            b = cf[2, mine + e, at]
            gradient[0, e, at] = (a * q_h + b * q_x + q_z) * F32(1.0 / 12.0)
            gradient[1, e, at] = c * q_h
            gradient[2, e, at] = c * q_x
        return carry

    lax.fori_loop(0, AX // 16, finish, 0)

    for copy in (send_up0, send_down0, send_up1, send_down1, send_sib, hop_up, hop_down):
        copy.wait_send()
    for copy in (pass_up0, pass_down0, pass_up1, pass_down1, pass_far0, pass_far1):
        copy.wait_send()
    for copy in (to_up0, to_down0, to_up1, to_down1, to_up2, to_down2):
        copy.wait_send()
    wait_send(functools.partial(whole, 3, 0))
    out_p.wait()
    out_q.wait()
    out_l.wait()
    out_m.wait()


def solution(mesh):
    n_shot, n_tile = mesh.shape["shot"], mesh.shape["tile"]

    def per_device(coefs, fwd_state, adj_state, src_cell, src_wave, rec_cells, observed):
        hbm = pl.BlockSpec(memory_space=pltpu.HBM)
        smem = pl.BlockSpec(memory_space=pltpu.SMEM)
        vmem = pl.BlockSpec(memory_space=pltpu.VMEM)
        dma = pltpu.SemaphoreType.DMA
        return pl.pallas_call(
            functools.partial(kernel, n_shot, n_tile),
            out_shape=(
                pltpu.VMEM((3, 2, AX, AY), F32),
                pltpu.VMEM((1, 2, AZ, AX, AY), F32),
                pltpu.VMEM((1, 2, AZ, AX, AY), F32),
            ),
            in_specs=[hbm, hbm, hbm, smem, smem, smem, vmem, hbm],
            out_specs=(vmem, vmem, vmem),
            scratch_shapes=[
                pltpu.VMEM((3, AZ, AX, AY), F32),
                pltpu.VMEM((2 * AZ, AX + 2 * PAD, AY), F32),
                pltpu.VMEM((2 * (AZ + 4), AX, AY), F32),
                pltpu.VMEM((STEPS * AZ, AX, AY), F32),
                pltpu.VMEM((STEPS * AZ, AX, AY), F32),
                pltpu.VMEM((2 * AZ, AX, AY), F32),
                pltpu.VMEM((2 * AZ, AX, AY), F32),
                pltpu.VMEM((2 * AZ, AX + 2 * PAD, AY), F32),
                pltpu.VMEM((2 * (AZ + 4), AX, AY), F32),
                pltpu.VMEM((3, AZ, AX, AY), F32),
                pltpu.VMEM((3, 8, AX, AY), F32),
                pltpu.VMEM((3, 6, AX, AY), F32),
                pltpu.VMEM((2 * 192, AY), F32),
                pltpu.VMEM((2 * 192, AY), F32),
                pltpu.VMEM((AZ * AX, 2 * NREC), jnp.bfloat16),
                pltpu.VMEM((STEPS + 1, NREC, AY), F32),
                pltpu.VMEM((8 * NREC, AY), jnp.bfloat16),
                pltpu.VMEM((2 * AX, AY), F32),
                pltpu.VMEM((2 * AX, AY), F32),
                pltpu.SMEM((STEPS, 1, NREC), F32),
                dma((10,)),
                dma((4,)),
                dma((2, 6, 4)),
                dma((2, 6, 4)),
                dma((2, 1)),
                dma((2, 1)),
                dma((13,)),
                dma((13,)),
                dma((10,)),
                dma((10,)),
            ],
            compiler_params=pltpu.CompilerParams(
                collective_id=0, has_side_effects=True, vmem_limit_bytes=56 * 1024 * 1024
            ),
        )(coefs, fwd_state, adj_state, src_cell, src_wave, rec_cells, rec_cells, observed.transpose(1, 0, 2))

    placed = (
        P(None, "shot", "tile", None),
        P("shot", None, None, "tile", None),
        P("shot", None, None, "tile", None),
        P("shot", "tile"),
        P("shot", None),
        P("shot", "tile"),
        P("shot", None, "tile"),
    )
    return jax.shard_map(
        per_device,
        mesh=mesh,
        in_specs=placed,
        out_specs=(
            P(None, "shot", "tile", None),
            P("shot", None, None, "tile", None),
            P("shot", None, None, "tile", None),
        ),
        check_vma=False,
    )
```

```python
import functools

import jax
import jax.numpy as jnp
from jax import lax
from jax.experimental import pallas as pl
from jax.experimental.pallas import tpu as pltpu
from jax.sharding import PartitionSpec as P

MESH = pl.DeviceIdType.MESH
F32 = jnp.float32
AZ, AX, AY, STEPS, NREC = 16, 128, 128, 6, 128
PAD = 8
GROUPS, DEEP, BATCH, SENDS = 4, 4, 4, 4
PER = GROUPS // SENDS
SPAN = 8 * PER


def kernel(
    n_shot,
    n_tile,
    coefs,
    fwd_state,
    adj_state,
    src_cell,
    src_wave,
    rec_cells,
    rec_row,
    observed_in,
    gradient,
    fwd_final,
    adj_final,
    cf,
    pp,
    qq,
    hs,
    zs,
    ll,
    mm,
    ff,
    oo,
    acc,
    rb,
    ry,
    hb,
    sb,
    picks,
    gath,
    spread,
    terms_a,
    terms_b,
    observed,
    load_sem,
    out_sem,
    halo_send,
    halo_recv,
    whole_send,
    whole_recv,
    ag_send,
    ag_recv,
    rs_send,
    rs_recv,
):
    shot = lax.axis_index("shot")
    tile = lax.axis_index("tile")
    chip = shot // 2
    core = shot % 2
    sibling = chip * 2 + (1 - core)
    up = (shot + 2) % n_shot
    down = (shot + n_shot - 2) % n_shot
    left = (tile + n_tile - 1) % n_tile
    right = (tile + 1) % n_tile
    has_left = tile > 0
    has_right = tile < n_tile - 1
    mine = 2 * shot
    mine_sib = 2 * sibling
    above = (mine + 4) % AZ
    below = (mine + 12) % AZ
    far = (mine + 8) % AZ
    above_sib = (mine_sib + 4) % AZ
    below_sib = (mine_sib + 12) % AZ
    far_sib = (mine_sib + 8) % AZ

    own_load = pltpu.make_async_copy(coefs, cf.at[:, pl.ds(mine, 2)], load_sem.at[0])
    own_load.start()
    observed_load = pltpu.make_async_copy(observed_in, observed, load_sem.at[9])
    observed_load.start()
    body = pl.ds(PAD, AX)
    loads = []
    for i, (src, dst) in enumerate(
        (
            (fwd_state.at[0, 0], pp.at[0:AZ, body]),
            (fwd_state.at[0, 1], qq.at[2 : AZ + 2]),
            (fwd_state.at[0, 2], pp.at[AZ : 2 * AZ, body]),
            (fwd_state.at[0, 3], qq.at[AZ + 6 : 2 * AZ + 6]),
            (adj_state.at[0, 0], ll.at[0:AZ]),
            (adj_state.at[0, 1], mm.at[0:AZ]),
            (adj_state.at[0, 2], ll.at[AZ : 2 * AZ]),
            (adj_state.at[0, 3], mm.at[AZ : 2 * AZ]),
        )
    ):
        loads.append(pltpu.make_async_copy(src, dst, load_sem.at[1 + i]))

    def clear(i, carry):
        hb[pl.ds(i * 32, 32)] = jnp.zeros((32, AY), F32)
        return carry

    lax.fori_loop(0, 12, clear, 0)

    barrier = pltpu.get_barrier_semaphore()
    for other in (sibling, up, down):
        pl.semaphore_signal(barrier, inc=1, device_id=(other, tile), device_id_type=MESH)

    @pl.when(has_left)
    def _():
        pl.semaphore_signal(barrier, inc=1, device_id=(shot, left), device_id_type=MESH)

    @pl.when(has_right)
    def _():
        pl.semaphore_signal(barrier, inc=1, device_id=(shot, right), device_id_type=MESH)

    for copy in loads:
        copy.start()
    own_load.wait()
    cf[0, pl.ds(mine, 2)] = cf[0, pl.ds(mine, 2)] * F32(1.0 / 12.0)

    pl.semaphore_wait(barrier, 3 + jnp.minimum(tile, 1) + jnp.minimum(n_tile - 1 - tile, 1))

    def ag(index, layer, count, target):
        part = cf.at[:, pl.ds(layer, count)]
        return pltpu.make_async_remote_copy(
            src_ref=part,
            dst_ref=part,
            send_sem=ag_send.at[index],
            recv_sem=ag_recv.at[index],
            device_id=(target, tile),
            device_id_type=MESH,
        )

    send_up0 = ag(1, mine, 1, up)
    send_up1 = ag(2, mine + 1, 1, up)
    send_down0 = ag(3, mine + 1, 1, down)
    send_down1 = ag(4, mine, 1, down)
    send_sib = ag(0, mine, 2, sibling)
    for copy in (send_up0, send_down0, send_up1, send_down1, send_sib):
        copy.start()
    got_up0 = ag(1, below, 1, up)
    got_up1 = ag(2, below + 1, 1, up)
    got_down0 = ag(3, above + 1, 1, down)
    got_down1 = ag(4, above, 1, down)
    hop_up = ag(5, below, 1, up)
    hop_down = ag(6, above + 1, 1, down)
    got_hop_up = ag(5, far, 1, up)
    got_hop_down = ag(6, far + 1, 1, down)
    got_sib = ag(0, mine_sib, 2, sibling)
    pass_up0 = ag(7, below, 1, sibling)
    pass_down0 = ag(8, above + 1, 1, sibling)
    pass_up1 = ag(9, below + 1, 1, sibling)
    pass_down1 = ag(10, above, 1, sibling)
    pass_far0 = ag(11, far, 1, sibling)
    pass_far1 = ag(12, far + 1, 1, sibling)
    via_up0 = ag(7, below_sib, 1, sibling)
    via_down0 = ag(8, above_sib + 1, 1, sibling)
    via_up1 = ag(9, below_sib + 1, 1, sibling)
    via_down1 = ag(10, above_sib, 1, sibling)
    via_far0 = ag(11, far_sib, 1, sibling)
    via_far1 = ag(12, far_sib + 1, 1, sibling)

    none = jnp.zeros((AX, AY), F32)
    for base in (0, AZ + 4):
        for extra in (0, 1, AZ + 2, AZ + 3):
            qq[base + extra] = none
            oo[base + extra] = none

    marked = rec_row[...] >> 7
    gap = lax.broadcasted_iota(jnp.int32, (AY, AY), 0) - lax.broadcasted_iota(jnp.int32, (AY, AY), 1)
    gap = gap * gap
    taps = jnp.where(gap == 0, F32(-60), F32(0)) + jnp.where(gap == 1, F32(16), F32(0)) - jnp.where(gap == 4, F32(1), F32(0))
    taps = taps.astype(jnp.bfloat16)
    for k in (2, 3, 6, 7):
        spread[k * NREC : (k + 1) * NREC] = taps

    def mark(i, carry):
        rows = lax.broadcasted_iota(jnp.int32, (16, NREC), 0) + i * 16
        hit = jnp.where(rows == marked, F32(1.0), F32(0.0)).astype(jnp.bfloat16)
        at = pl.ds(pl.multiple_of(i * 16, 16), 16)
        picks[at, 0:NREC] = hit
        picks[at, NREC : 2 * NREC] = hit
        return carry

    lax.fori_loop(0, AZ * AX // 16, mark, 0)

    def halo(slot, group, to_right):
        src = sb.at[pl.ds((1 if to_right else 0) * 192 + slot * 32 + group * SPAN, SPAN)]
        dst = hb.at[pl.ds((0 if to_right else 1) * 192 + slot * 32 + group * SPAN, SPAN)]
        side = 0 if to_right else 1
        return pltpu.make_async_remote_copy(
            src_ref=src,
            dst_ref=dst,
            send_sem=halo_send.at[side, slot],
            recv_sem=halo_recv.at[side, slot, group],
            device_id=(shot, right if to_right else left),
            device_id_type=MESH,
        )

    def sent(slot, to_right):
        rows = pl.ds((1 if to_right else 0) * 192 + slot * 32, 32)
        side = 0 if to_right else 1
        return pltpu.make_async_remote_copy(
            src_ref=sb.at[rows],
            dst_ref=hb.at[rows],
            send_sem=halo_send.at[side, slot],
            recv_sem=halo_recv.at[side, slot, 0],
            device_id=(shot, right if to_right else left),
            device_id_type=MESH,
        )

    def whole(slot, index, to_right):
        src = sb.at[pl.ds((1 if to_right else 0) * 192 + slot * 32, 32)]
        dst = hb.at[pl.ds((0 if to_right else 1) * 192 + slot * 32, 32)]
        side = 0 if to_right else 1
        return pltpu.make_async_remote_copy(
            src_ref=src,
            dst_ref=dst,
            send_sem=whole_send.at[side, index],
            recv_sem=whole_recv.at[side, index],
            device_id=(shot, right if to_right else left),
            device_id_type=MESH,
        )

    def both(build, act_left, act_right):
        @pl.when(has_left)
        def _():
            act_left(build)

        @pl.when(has_right)
        def _():
            act_right(build)

    def start(build):
        both(build, lambda b: b(False).start(), lambda b: b(True).start())

    def wait_send(build):
        both(build, lambda b: b(False).wait_send(), lambda b: b(True).wait_send())

    def wait_recv(build):
        both(build, lambda b: b(True).wait_recv(), lambda b: b(False).wait_recv())

    def ready(slot, i):
        @pl.when(i % PER == PER - 1)
        def _():
            start(functools.partial(halo, slot, i // PER))

    def arrived(slot, i):
        @pl.when(i % PER == 0)
        def _():
            wait_recv(functools.partial(halo, slot, i // PER))

    def stage_rows(field, at, slot, layer):
        sb[pl.ds(slot * 32 + layer * 2, 2)] = field[at, PAD : PAD + 2]
        sb[pl.ds(192 + slot * 32 + layer * 2, 2)] = field[at, PAD + AX - 2 : PAD + AX]

    def land_rows(field, at, slot, layer):
        field[at, PAD - 2 : PAD] = hb[pl.ds(slot * 32 + layer * 2, 2)]
        field[at, PAD + AX : PAD + AX + 2] = hb[pl.ds(192 + slot * 32 + layer * 2, 2)]

    loads[0].wait()

    def ring_place(i):
        return (chip + i + i // 2 - 2 * (i // 3)) % GROUPS

    def stage_first(i, carry):
        stage_rows(pp, ring_place(i // DEEP) * DEEP + i % DEEP, 3, i)
        return carry

    lax.fori_loop(0, AZ, stage_first, 0)
    start(functools.partial(whole, 3, 0))

    lane = lax.broadcasted_iota(jnp.int32, (1, AY), 1)
    flat = lax.broadcasted_iota(jnp.int32, (8, AY), 0) * AY + lax.broadcasted_iota(jnp.int32, (8, AY), 1)
    source = src_cell[0, 0]

    def lap(field, at, r):
        def rows(k):
            return field[at, r + k : r + k + 8]

        return F32(16) * (rows(-1) + rows(1)) - (rows(-2) + rows(2))

    def deep(layers):
        return F32(16) * (layers[1] + layers[3]) - (layers[0] + layers[4]) - F32(30) * layers[2]

    def flat_terms(field, parity, d, out, side):
        value = field[pl.ds(parity * AZ + d, 2), PAD : PAD + AX].reshape(2 * AX, AY)
        high = value.astype(jnp.bfloat16)
        low = (value - high.astype(F32)).astype(jnp.bfloat16)
        if side is None:
            left_side = jnp.concatenate([high, low], axis=1)
            out[...] = jnp.dot(left_side, spread[2 * NREC : 4 * NREC], preferred_element_type=F32)
        else:
            hits = picks[pl.ds(pl.multiple_of(d * AX, AX), 2 * AX)]
            left_side = jnp.concatenate([hits, high, low], axis=1)
            right_side = spread[pl.ds(pl.multiple_of(side * 4 * NREC, 4 * NREC), 4 * NREC)]
            out[...] = jnp.dot(left_side, right_side, preferred_element_type=F32)

    def gather_row(slot, parity, r, at_obs):
        cell = rec_cells[0, r]
        col = cell & (AY - 1)
        line = pp[parity * AZ + (cell >> 14), pl.ds(PAD + ((cell >> 7) & (AX - 1)), 1)]
        line = line - observed[at_obs, 0, r]
        gath[slot, pl.ds(r, 1)] = jnp.where(lane == col, line, F32(0))

    def flush(done, t):
        if t % BATCH == BATCH - 1:
            for field, layer, at, value in done:
                field[layer, at] = value
            done.clear()

    def forward_pair(n, cur, d, terms):
        nxt = 1 - cur
        here = cur * AZ + d
        there = nxt * AZ + d
        q_here = cur * (AZ + 4) + d
        q_there = nxt * (AZ + 4) + d + 2
        wave = src_wave[0, n]
        start_cell = source - d * (AX * AY)
        done = []
        for t in range(AX // 8):
            r = PAD + 8 * t
            at = slice(8 * t, 8 * t + 8)
            layers = [qq[q_here + k, at] for k in range(6)]
            for e in range(2):
                c = cf[0, d + e, at]
                a = cf[1, d + e, at]
                b = cf[2, d + e, at]
                h = lap(pp, here + e, r) + terms[e * AX + 8 * t : e * AX + 8 * t + 8]
                z = deep(layers[e : e + 5])
                done.append((hs, n * AZ + d + e, at, h))
                done.append((zs, n * AZ + d + e, at, z))
                pulse = jnp.where(flat == start_cell - (AX * AY * e + 1024 * t), wave, F32(0))
                p = pp[here + e, r : r + 8]
                q = layers[e + 2]
                p_new = (p + p) - pp[there + e, r : r + 8] + c * (a * h + b * z) + pulse
                q_new = (q + q) - qq[q_there + e, at] + c * (b * h + z) + pulse
                done.append((pp, there + e, slice(r, r + 8), p_new))
                done.append((qq, q_there + e, at, q_new))
            flush(done, t)

    def scaled_pair(d):
        for t in range(AX // 8):
            r = PAD + 8 * t
            at = slice(8 * t, 8 * t + 8)
            for e in range(2):
                c = cf[0, d + e, at]
                a = cf[1, d + e, at]
                b = cf[2, d + e, at]
                lam = ll[d + e, at]
                mu = mm[d + e, at]
                ff[d + e, r : r + 8] = c * (a * lam + b * mu)
                oo[d + e + 2, at] = c * (b * lam + mu)

    def forward_group(n, cur, i, group, slot):
        d = group * DEEP
        for e in range(DEEP):
            land_rows(pp, cur * AZ + d + e, slot, i * DEEP + e)
        after = (cur + (i + 1) // GROUPS) % 2
        obs_at = jnp.maximum(n - 1, 0)
        flat_terms(pp, cur, d + 2, terms_b, None)
        for j in range(16):
            gather_row(n, cur, i * 32 + j, obs_at)
        forward_pair(n, cur, d, terms_a)
        flat_terms(pp, after, ring_place((i + 1) % GROUPS) * DEEP, terms_a, None)
        for j in range(16, 32):
            gather_row(n, cur, i * 32 + j, obs_at)
        forward_pair(n, cur, d + 2, terms_b)
        for e in range(DEEP):
            stage_rows(pp, (1 - cur) * AZ + d + e, 1 - cur, i * DEEP + e)

    flat_terms(pp, 0, ring_place(0) * DEEP, terms_a, None)
    observed_load.wait()
    for i in range(1, 8):
        loads[i].wait()
    wait_recv(functools.partial(whole, 3, 0))
    got_sib.wait_recv()

    def first_group(i, carry):
        @pl.when(i == 1)
        def _():
            got_up0.wait_recv()
            hop_up.start()
            pass_up0.start()
            got_down0.wait_recv()
            hop_down.start()
            pass_down0.start()
            got_up1.wait_recv()
            pass_up1.start()
            got_down1.wait_recv()
            pass_down1.start()
            via_down0.wait_recv()
            via_down1.wait_recv()

        @pl.when(i == 2)
        def _():
            via_up0.wait_recv()
            via_up1.wait_recv()

        @pl.when(i == 3)
        def _():
            got_hop_up.wait_recv()
            pass_far0.start()
            got_hop_down.wait_recv()
            pass_far1.start()
            via_far0.wait_recv()
            via_far1.wait_recv()

        group = ring_place(i)
        d = group * DEEP
        forward_group(0, 0, i, group, 3)
        ready(1, i)
        scaled_pair(d)
        scaled_pair(d + 2)
        for e in range(DEEP):
            stage_rows(ff, d + e, 4, i * DEEP + e)
        ready(4, i)
        return carry

    lax.fori_loop(0, GROUPS, first_group, 0)

    def forward_step(n, carry):
        cur = n % 2

        def one_group(i, carry):
            group = ring_place(i)
            arrived(cur, i)
            forward_group(n, cur, i, group, cur)

            @pl.when(n < STEPS - 1)
            def _():
                ready(1 - cur, i)

            return carry

        lax.fori_loop(0, GROUPS, one_group, 0)
        wait_send(functools.partial(sent, cur))
        return carry

    lax.fori_loop(1, STEPS, forward_step, 0)

    out_p = pltpu.make_async_copy(pp.at[0:AZ, body], fwd_final.at[0, 0], out_sem.at[0])
    out_q = pltpu.make_async_copy(qq.at[2 : AZ + 2], fwd_final.at[0, 1], out_sem.at[1])
    out_p.start()
    out_q.start()

    def gather_last(i, carry):
        for j in range(16):
            gather_row(STEPS, 0, i * 16 + j, STEPS - 1)
        return carry

    lax.fori_loop(0, NREC // 16, gather_last, 0)

    def adj_pair(s, cur, d, terms, mode):
        nxt = 1 - cur
        here = cur * AZ + d
        there = nxt * AZ + d
        o_here = cur * (AZ + 4) + d
        o_there = nxt * (AZ + 4) + d + 2
        k = STEPS - s
        done = []
        for t in range(AX // 8):
            r = PAD + 8 * t
            at = slice(8 * t, 8 * t + 8)
            layers = [oo[o_here + n, at] for n in range(6)]
            for e in range(2):
                lam = ll[here + e, at]
                mu = mm[here + e, at]
                lam_old = ll[there + e, at]
                mu_old = mm[there + e, at]
                mix = terms[e * AX + 8 * t : e * AX + 8 * t + 8]
                lam_new = (lam + lam) - lam_old + lap(ff, here + e, r) + mix
                mu_new = (mu + mu) - mu_old + deep(layers[e : e + 5])
                done.append((ll, there + e, at, lam_new))
                done.append((mm, there + e, at, mu_new))
                if mode != "last":
                    c = cf[0, d + e, at]
                    a = cf[1, d + e, at]
                    b = cf[2, d + e, at]
                    done.append((ff, there + e, slice(r, r + 8), c * (a * lam_new + b * mu_new)))
                    done.append((oo, o_there + e, at, c * (b * lam_new + mu_new)))
                if mode != "plain":
                    h0 = hs[(k - 1) * AZ + d + e, at]
                    z0 = zs[(k - 1) * AZ + d + e, at]
                    h1 = hs[k * AZ + d + e, at]
                    z1 = zs[k * AZ + d + e, at]
                    h2 = hs[(k + 1) * AZ + d + e, at]
                    z2 = zs[(k + 1) * AZ + d + e, at]
                    q_h = lam_new * h0 + lam * h1 + lam_old * h2
                    q_x = (lam_new * z0 + mu_new * h0) + (lam * z1 + mu * h1) + (lam_old * z2 + mu_old * h2)
                    q_z = mu_new * z0 + mu * z1 + mu_old * z2
                    if mode == "last":
                        q_h += acc[0, d + e, at]
                        q_x += acc[1, d + e, at]
                        q_z += acc[2, d + e, at]
                    done.append((acc.at[0], d + e, at, q_h))
                    done.append((acc.at[1], d + e, at, q_x))
                    done.append((acc.at[2], d + e, at, q_z))
            flush(done, t)

    def set_spread(k, side):
        value = gath[k]
        high = value.astype(jnp.bfloat16)
        low = (value - high.astype(F32)).astype(jnp.bfloat16)
        base = pl.multiple_of(side * 4 * NREC, 4 * NREC)
        spread[pl.ds(base, 2 * NREC)] = jnp.concatenate([high, low], axis=0)

    def last_place(i):
        return (chip + 2 + i - 3 * (i // 2) - 2 * (i // 3)) % GROUPS

    def adj_group(s, cur, i, mode, place):
        group = place(i)
        d = group * DEEP
        slot = 4 + cur
        order = i if place is ring_place else GROUPS - 1 - i

        @pl.when(i % PER == 0)
        def _():
            wait_recv(functools.partial(halo, slot, order // PER))

        for e in range(DEEP):
            land_rows(ff, cur * AZ + d + e, slot, order * DEEP + e)
        flat_terms(ff, cur, d + 2, terms_b, cur)
        adj_pair(s, cur, d, terms_a, mode)
        flat_terms(ff, cur, place((i + 1) % GROUPS) * DEEP, terms_a, cur)
        adj_pair(s, cur, d + 2, terms_b, mode)
        if mode != "last":
            for e in range(DEEP):
                stage_rows(ff, (1 - cur) * AZ + d + e, 5 - cur, i * DEEP + e)
            ready(5 - cur, i)

    def adj_step(s, mode, carry):
        cur = s % 2
        set_spread(STEPS - s, cur)
        flat_terms(ff, cur, ring_place(0) * DEEP, terms_a, cur)

        def one_group(i, carry):
            adj_group(s, cur, i, mode, ring_place)
            return carry

        lax.fori_loop(0, GROUPS, one_group, 0)
        wait_send(functools.partial(sent, 4 + cur))
        return carry

    lax.fori_loop(0, 2, lambda s, carry: adj_step(s, "plain", carry), 0)
    adj_step(2, "third", 0)
    lax.fori_loop(3, 5, lambda s, carry: adj_step(s, "plain", carry), 0)

    def exchange(i, group):
        layer = group * DEEP
        return pltpu.make_async_remote_copy(
            src_ref=acc.at[:, pl.ds(layer + 2 * (1 - core), 2)],
            dst_ref=rb.at[:, pl.ds(2 * i, 2)],
            send_sem=rs_send.at[i],
            recv_sem=rs_recv.at[i],
            device_id=(sibling, tile),
            device_id_type=MESH,
        )

    def ring(index, layer, target):
        return pltpu.make_async_remote_copy(
            src_ref=acc.at[:, pl.ds(layer, 1)],
            dst_ref=ry.at[:, pl.ds(index, 1)],
            send_sem=rs_send.at[4 + index],
            recv_sem=rs_recv.at[4 + index],
            device_id=(target, tile),
            device_id_type=MESH,
        )

    def add_pair(i, group):
        layer = group * DEEP + 2 * core

        def add(t, carry):
            at = pl.ds(pl.multiple_of(t * 16, 16), 16)
            for f in range(3):
                for e in range(2):
                    acc[f, layer + e, at] = acc[f, layer + e, at] + rb[f, 2 * i + e, at]
            return carry

        lax.fori_loop(0, AX // 16, add, 0)

    def add_hop(index, layer):
        def add(t, carry):
            at = pl.ds(pl.multiple_of(t * 16, 16), 16)
            for f in range(3):
                acc[f, layer, at] = acc[f, layer, at] + ry[f, index, at]
            return carry

        lax.fori_loop(0, AX // 16, add, 0)

    to_up0 = ring(0, far, up)
    to_down0 = ring(1, far + 1, down)
    to_up1 = ring(2, above + 1, up)
    to_down1 = ring(3, below, down)
    to_up2 = ring(4, above, up)
    to_down2 = ring(5, below + 1, down)

    set_spread(1, 1)
    flat_terms(ff, 1, last_place(0) * DEEP, terms_a, 1)

    def swap(i):
        return exchange(i, last_place(i))

    def summed(i):
        swap(i).wait_send()
        swap(i).wait_recv()
        add_pair(i, last_place(i))

    def last_group(i, carry):
        adj_group(5, 1, i, "last", last_place)
        swap(i).start()

        @pl.when(i > 0)
        def _():
            summed(i - 1)

        @pl.when(i == 1)
        def _():
            to_up0.start()
            to_down0.start()

        @pl.when(i == 2)
        def _():
            to_down1.start()

        @pl.when(i == 3)
        def _():
            to_up1.start()

        return carry

    lax.fori_loop(0, GROUPS, last_group, 0)
    out_l = pltpu.make_async_copy(ll.at[0:AZ], adj_final.at[0, 0], out_sem.at[2])
    out_m = pltpu.make_async_copy(mm.at[0:AZ], adj_final.at[0, 1], out_sem.at[3])
    out_l.start()
    out_m.start()
    summed(GROUPS - 1)
    to_up0.wait_recv()
    add_hop(0, above)
    to_up2.start()
    to_down0.wait_recv()
    add_hop(1, below + 1)
    to_down2.start()
    to_up1.wait_recv()
    to_down1.wait_recv()
    to_up2.wait_recv()
    to_down2.wait_recv()

    def finish(t, carry):
        at = pl.ds(pl.multiple_of(t * 16, 16), 16)
        for e, (direct, passed) in enumerate(((3, 4), (2, 5))):
            q_h, q_x, q_z = (
                acc[f, mine + e, at] + ry[f, direct, at] + ry[f, passed, at] for f in range(3)
            )
            c = cf[0, mine + e, at]
            a = cf[1, mine + e, at]
            b = cf[2, mine + e, at]
            gradient[0, e, at] = (a * q_h + b * q_x + q_z) * F32(1.0 / 12.0)
            gradient[1, e, at] = c * q_h
            gradient[2, e, at] = c * q_x
        return carry

    lax.fori_loop(0, AX // 16, finish, 0)

    for copy in (send_up0, send_down0, send_up1, send_down1, send_sib, hop_up, hop_down):
        copy.wait_send()
    for copy in (pass_up0, pass_down0, pass_up1, pass_down1, pass_far0, pass_far1):
        copy.wait_send()
    for copy in (to_up0, to_down0, to_up1, to_down1, to_up2, to_down2):
        copy.wait_send()
    wait_send(functools.partial(whole, 3, 0))
    wait_send(functools.partial(sent, 5))
    out_p.wait()
    out_q.wait()
    out_l.wait()
    out_m.wait()


def solution(mesh):
    n_shot, n_tile = mesh.shape["shot"], mesh.shape["tile"]

    def per_device(coefs, fwd_state, adj_state, src_cell, src_wave, rec_cells, observed):
        hbm = pl.BlockSpec(memory_space=pltpu.HBM)
        smem = pl.BlockSpec(memory_space=pltpu.SMEM)
        vmem = pl.BlockSpec(memory_space=pltpu.VMEM)
        dma = pltpu.SemaphoreType.DMA
        return pl.pallas_call(
            functools.partial(kernel, n_shot, n_tile),
            out_shape=(
                pltpu.VMEM((3, 2, AX, AY), F32),
                pltpu.VMEM((1, 2, AZ, AX, AY), F32),
                pltpu.VMEM((1, 2, AZ, AX, AY), F32),
            ),
            in_specs=[hbm, hbm, hbm, smem, smem, smem, vmem, hbm],
            out_specs=(vmem, vmem, vmem),
            scratch_shapes=[
                pltpu.VMEM((3, AZ, AX, AY), F32),
                pltpu.VMEM((2 * AZ, AX + 2 * PAD, AY), F32),
                pltpu.VMEM((2 * (AZ + 4), AX, AY), F32),
                pltpu.VMEM((STEPS * AZ, AX, AY), F32),
                pltpu.VMEM((STEPS * AZ, AX, AY), F32),
                pltpu.VMEM((2 * AZ, AX, AY), F32),
                pltpu.VMEM((2 * AZ, AX, AY), F32),
                pltpu.VMEM((2 * AZ, AX + 2 * PAD, AY), F32),
                pltpu.VMEM((2 * (AZ + 4), AX, AY), F32),
                pltpu.VMEM((3, AZ, AX, AY), F32),
                pltpu.VMEM((3, 8, AX, AY), F32),
                pltpu.VMEM((3, 6, AX, AY), F32),
                pltpu.VMEM((2 * 192, AY), F32),
                pltpu.VMEM((2 * 192, AY), F32),
                pltpu.VMEM((AZ * AX, 2 * NREC), jnp.bfloat16),
                pltpu.VMEM((STEPS + 1, NREC, AY), F32),
                pltpu.VMEM((8 * NREC, AY), jnp.bfloat16),
                pltpu.VMEM((2 * AX, AY), F32),
                pltpu.VMEM((2 * AX, AY), F32),
                pltpu.SMEM((STEPS, 1, NREC), F32),
                dma((10,)),
                dma((4,)),
                dma((2, 6)),
                dma((2, 6, 4)),
                dma((2, 1)),
                dma((2, 1)),
                dma((13,)),
                dma((13,)),
                dma((10,)),
                dma((10,)),
            ],
            compiler_params=pltpu.CompilerParams(
                collective_id=0, has_side_effects=True, vmem_limit_bytes=56 * 1024 * 1024
            ),
        )(coefs, fwd_state, adj_state, src_cell, src_wave, rec_cells, rec_cells, observed.transpose(1, 0, 2))

    placed = (
        P(None, "shot", "tile", None),
        P("shot", None, None, "tile", None),
        P("shot", None, None, "tile", None),
        P("shot", "tile"),
        P("shot", None),
        P("shot", "tile"),
        P("shot", None, "tile"),
    )
    return jax.shard_map(
        per_device,
        mesh=mesh,
        in_specs=placed,
        out_specs=(
            P(None, "shot", "tile", None),
            P("shot", None, None, "tile", None),
            P("shot", None, None, "tile", None),
        ),
        check_vma=False,
    )
```

```python
import functools

import jax
import jax.numpy as jnp
from jax import lax
from jax.experimental import pallas as pl
from jax.experimental.pallas import tpu as pltpu
from jax.sharding import PartitionSpec as P

MESH = pl.DeviceIdType.MESH
F32 = jnp.float32
AZ, AX, AY, STEPS, NREC = 16, 128, 128, 6, 128
PAD = 8
GROUPS, DEEP, BATCH, SENDS = 4, 4, 4, 4
PER = GROUPS // SENDS
SPAN = 8 * PER


def kernel(
    n_shot,
    n_tile,
    coefs,
    fwd_state,
    adj_state,
    src_cell,
    src_wave,
    rec_cells,
    rec_row,
    observed_in,
    gradient,
    fwd_final,
    adj_final,
    cf,
    pp,
    qq,
    hs,
    zs,
    ll,
    mm,
    ff,
    oo,
    acc,
    rb,
    ry,
    hb,
    sb,
    picks,
    gath,
    spread,
    terms_a,
    terms_b,
    observed,
    load_sem,
    out_sem,
    halo_send,
    halo_recv,
    whole_send,
    whole_recv,
    ag_send,
    ag_recv,
    rs_send,
    rs_recv,
):
    shot = lax.axis_index("shot")
    tile = lax.axis_index("tile")
    chip = shot // 2
    core = shot % 2
    sibling = chip * 2 + (1 - core)
    up = (shot + 2) % n_shot
    down = (shot + n_shot - 2) % n_shot
    left = (tile + n_tile - 1) % n_tile
    right = (tile + 1) % n_tile
    has_left = tile > 0
    has_right = tile < n_tile - 1
    mine = 2 * shot
    mine_sib = 2 * sibling
    above = (mine + 4) % AZ
    below = (mine + 12) % AZ
    far = (mine + 8) % AZ
    above_sib = (mine_sib + 4) % AZ
    below_sib = (mine_sib + 12) % AZ
    far_sib = (mine_sib + 8) % AZ

    own_load = pltpu.make_async_copy(coefs, cf.at[:, pl.ds(mine, 2)], load_sem.at[0])
    own_load.start()
    observed_load = pltpu.make_async_copy(observed_in, observed, load_sem.at[9])
    observed_load.start()
    body = pl.ds(PAD, AX)
    loads = []
    for i, (src, dst) in enumerate(
        (
            (fwd_state.at[0, 0], pp.at[0:AZ, body]),
            (fwd_state.at[0, 1], qq.at[2 : AZ + 2]),
            (fwd_state.at[0, 2], pp.at[AZ : 2 * AZ, body]),
            (fwd_state.at[0, 3], qq.at[AZ + 6 : 2 * AZ + 6]),
            (adj_state.at[0, 0], ll.at[0:AZ]),
            (adj_state.at[0, 1], mm.at[0:AZ]),
            (adj_state.at[0, 2], ll.at[AZ : 2 * AZ]),
            (adj_state.at[0, 3], mm.at[AZ : 2 * AZ]),
        )
    ):
        loads.append(pltpu.make_async_copy(src, dst, load_sem.at[1 + i]))

    def clear(i, carry):
        hb[pl.ds(i * 32, 32)] = jnp.zeros((32, AY), F32)
        return carry

    lax.fori_loop(0, 12, clear, 0)

    barrier = pltpu.get_barrier_semaphore()
    for other in (sibling, up, down):
        pl.semaphore_signal(barrier, inc=1, device_id=(other, tile), device_id_type=MESH)

    @pl.when(has_left)
    def _():
        pl.semaphore_signal(barrier, inc=1, device_id=(shot, left), device_id_type=MESH)

    @pl.when(has_right)
    def _():
        pl.semaphore_signal(barrier, inc=1, device_id=(shot, right), device_id_type=MESH)

    for copy in loads:
        copy.start()
    own_load.wait()
    cf[0, pl.ds(mine, 2)] = cf[0, pl.ds(mine, 2)] * F32(1.0 / 12.0)

    pl.semaphore_wait(barrier, 3 + jnp.minimum(tile, 1) + jnp.minimum(n_tile - 1 - tile, 1))

    def ag(index, layer, count, target):
        part = cf.at[:, pl.ds(layer, count)]
        return pltpu.make_async_remote_copy(
            src_ref=part,
            dst_ref=part,
            send_sem=ag_send.at[index],
            recv_sem=ag_recv.at[index],
            device_id=(target, tile),
            device_id_type=MESH,
        )

    send_up0 = ag(1, mine, 1, up)
    send_up1 = ag(2, mine + 1, 1, up)
    send_down0 = ag(3, mine + 1, 1, down)
    send_down1 = ag(4, mine, 1, down)
    send_sib = ag(0, mine, 2, sibling)
    for copy in (send_up0, send_down0, send_up1, send_down1, send_sib):
        copy.start()
    got_up0 = ag(1, below, 1, up)
    got_up1 = ag(2, below + 1, 1, up)
    got_down0 = ag(3, above + 1, 1, down)
    got_down1 = ag(4, above, 1, down)
    hop_up = ag(5, below, 1, up)
    hop_down = ag(6, above + 1, 1, down)
    got_hop_up = ag(5, far, 1, up)
    got_hop_down = ag(6, far + 1, 1, down)
    got_sib = ag(0, mine_sib, 2, sibling)
    pass_up0 = ag(7, below, 1, sibling)
    pass_down0 = ag(8, above + 1, 1, sibling)
    pass_up1 = ag(9, below + 1, 1, sibling)
    pass_down1 = ag(10, above, 1, sibling)
    pass_far0 = ag(11, far, 1, sibling)
    pass_far1 = ag(12, far + 1, 1, sibling)
    via_up0 = ag(7, below_sib, 1, sibling)
    via_down0 = ag(8, above_sib + 1, 1, sibling)
    via_up1 = ag(9, below_sib + 1, 1, sibling)
    via_down1 = ag(10, above_sib, 1, sibling)
    via_far0 = ag(11, far_sib, 1, sibling)
    via_far1 = ag(12, far_sib + 1, 1, sibling)

    none = jnp.zeros((AX, AY), F32)
    for base in (0, AZ + 4):
        for extra in (0, 1, AZ + 2, AZ + 3):
            qq[base + extra] = none
            oo[base + extra] = none

    marked = rec_row[...] >> 7
    gap = lax.broadcasted_iota(jnp.int32, (AY, AY), 0) - lax.broadcasted_iota(jnp.int32, (AY, AY), 1)
    gap = gap * gap
    taps = jnp.where(gap == 0, F32(-60), F32(0)) + jnp.where(gap == 1, F32(16), F32(0)) - jnp.where(gap == 4, F32(1), F32(0))
    taps = taps.astype(jnp.bfloat16)
    for k in (2, 3, 6, 7):
        spread[k * NREC : (k + 1) * NREC] = taps

    def mark(i, carry):
        rows = lax.broadcasted_iota(jnp.int32, (16, NREC), 0) + i * 16
        hit = jnp.where(rows == marked, F32(1.0), F32(0.0)).astype(jnp.bfloat16)
        at = pl.ds(pl.multiple_of(i * 16, 16), 16)
        picks[at, 0:NREC] = hit
        picks[at, NREC : 2 * NREC] = hit
        return carry

    lax.fori_loop(0, AZ * AX // 16, mark, 0)

    def halo(slot, group, to_right):
        src = sb.at[pl.ds((1 if to_right else 0) * 192 + slot * 32 + group * SPAN, SPAN)]
        dst = hb.at[pl.ds((0 if to_right else 1) * 192 + slot * 32 + group * SPAN, SPAN)]
        side = 0 if to_right else 1
        return pltpu.make_async_remote_copy(
            src_ref=src,
            dst_ref=dst,
            send_sem=halo_send.at[side, slot],
            recv_sem=halo_recv.at[side, slot, group],
            device_id=(shot, right if to_right else left),
            device_id_type=MESH,
        )

    def sent(slot, to_right):
        rows = pl.ds((1 if to_right else 0) * 192 + slot * 32, 32)
        side = 0 if to_right else 1
        return pltpu.make_async_remote_copy(
            src_ref=sb.at[rows],
            dst_ref=hb.at[rows],
            send_sem=halo_send.at[side, slot],
            recv_sem=halo_recv.at[side, slot, 0],
            device_id=(shot, right if to_right else left),
            device_id_type=MESH,
        )

    def whole(slot, index, to_right):
        src = sb.at[pl.ds((1 if to_right else 0) * 192 + slot * 32, 32)]
        dst = hb.at[pl.ds((0 if to_right else 1) * 192 + slot * 32, 32)]
        side = 0 if to_right else 1
        return pltpu.make_async_remote_copy(
            src_ref=src,
            dst_ref=dst,
            send_sem=whole_send.at[side, index],
            recv_sem=whole_recv.at[side, index],
            device_id=(shot, right if to_right else left),
            device_id_type=MESH,
        )

    def both(build, act_left, act_right):
        @pl.when(has_left)
        def _():
            act_left(build)

        @pl.when(has_right)
        def _():
            act_right(build)

    def start(build):
        both(build, lambda b: b(False).start(), lambda b: b(True).start())

    def wait_send(build):
        both(build, lambda b: b(False).wait_send(), lambda b: b(True).wait_send())

    def wait_recv(build):
        both(build, lambda b: b(True).wait_recv(), lambda b: b(False).wait_recv())

    def ready(slot, i):
        @pl.when(i % PER == PER - 1)
        def _():
            start(functools.partial(halo, slot, i // PER))

    def arrived(slot, i):
        @pl.when(i % PER == 0)
        def _():
            wait_recv(functools.partial(halo, slot, i // PER))

    def stage_rows(field, at, slot, layer):
        sb[pl.ds(slot * 32 + layer * 2, 2)] = field[at, PAD : PAD + 2]
        sb[pl.ds(192 + slot * 32 + layer * 2, 2)] = field[at, PAD + AX - 2 : PAD + AX]

    def land_rows(field, at, slot, layer):
        field[at, PAD - 2 : PAD] = hb[pl.ds(slot * 32 + layer * 2, 2)]
        field[at, PAD + AX : PAD + AX + 2] = hb[pl.ds(192 + slot * 32 + layer * 2, 2)]

    loads[0].wait()

    def ring_place(i):
        return (chip + i + i // 2 - 2 * (i // 3)) % GROUPS

    def stage_first(i, carry):
        stage_rows(pp, ring_place(i // DEEP) * DEEP + i % DEEP, 3, i)
        return carry

    lax.fori_loop(0, AZ, stage_first, 0)
    start(functools.partial(whole, 3, 0))

    lane = lax.broadcasted_iota(jnp.int32, (1, AY), 1)
    flat = lax.broadcasted_iota(jnp.int32, (8, AY), 0) * AY + lax.broadcasted_iota(jnp.int32, (8, AY), 1)
    source = src_cell[0, 0]

    def lap(field, at, r):
        def rows(k):
            return field[at, r + k : r + k + 8]

        return F32(16) * (rows(-1) + rows(1)) - (rows(-2) + rows(2))

    def deep(layers):
        return F32(16) * (layers[1] + layers[3]) - (layers[0] + layers[4]) - F32(30) * layers[2]

    def flat_terms(field, parity, d, out, side):
        value = field[pl.ds(parity * AZ + d, 2), PAD : PAD + AX].reshape(2 * AX, AY)
        high = value.astype(jnp.bfloat16)
        low = (value - high.astype(F32)).astype(jnp.bfloat16)
        if side is None:
            left_side = jnp.concatenate([high, low], axis=1)
            out[...] = jnp.dot(left_side, spread[2 * NREC : 4 * NREC], preferred_element_type=F32)
        else:
            hits = picks[pl.ds(pl.multiple_of(d * AX, AX), 2 * AX)]
            left_side = jnp.concatenate([hits, high, low], axis=1)
            right_side = spread[pl.ds(pl.multiple_of(side * 4 * NREC, 4 * NREC), 4 * NREC)]
            out[...] = jnp.dot(left_side, right_side, preferred_element_type=F32)

    def gather_row(slot, parity, r, at_obs):
        cell = rec_cells[0, r]
        col = cell & (AY - 1)
        line = pp[parity * AZ + (cell >> 14), pl.ds(PAD + ((cell >> 7) & (AX - 1)), 1)]
        line = line - observed[at_obs, 0, r]
        gath[slot, pl.ds(r, 1)] = jnp.where(lane == col, line, F32(0))

    def flush(done, t):
        if t % BATCH == BATCH - 1:
            for field, layer, at, value in done:
                field[layer, at] = value
            done.clear()

    def forward_pair(n, cur, d, terms):
        nxt = 1 - cur
        here = cur * AZ + d
        there = nxt * AZ + d
        q_here = cur * (AZ + 4) + d
        q_there = nxt * (AZ + 4) + d + 2
        wave = src_wave[0, n]
        start_cell = source - d * (AX * AY)
        done = []
        for t in range(AX // 8):
            r = PAD + 8 * t
            at = slice(8 * t, 8 * t + 8)
            layers = [qq[q_here + k, at] for k in range(6)]
            for e in range(2):
                c = cf[0, d + e, at]
                a = cf[1, d + e, at]
                b = cf[2, d + e, at]
                h = lap(pp, here + e, r) + terms[e * AX + 8 * t : e * AX + 8 * t + 8]
                z = deep(layers[e : e + 5])
                done.append((hs, n * AZ + d + e, at, h))
                done.append((zs, n * AZ + d + e, at, z))
                pulse = jnp.where(flat == start_cell - (AX * AY * e + 1024 * t), wave, F32(0))
                p = pp[here + e, r : r + 8]
                q = layers[e + 2]
                p_new = (p + p) - pp[there + e, r : r + 8] + c * (a * h + b * z) + pulse
                q_new = (q + q) - qq[q_there + e, at] + c * (b * h + z) + pulse
                done.append((pp, there + e, slice(r, r + 8), p_new))
                done.append((qq, q_there + e, at, q_new))
            flush(done, t)

    def scaled_pair(d):
        for t in range(AX // 8):
            r = PAD + 8 * t
            at = slice(8 * t, 8 * t + 8)
            for e in range(2):
                c = cf[0, d + e, at]
                a = cf[1, d + e, at]
                b = cf[2, d + e, at]
                lam = ll[d + e, at]
                mu = mm[d + e, at]
                ff[d + e, r : r + 8] = c * (a * lam + b * mu)
                oo[d + e + 2, at] = c * (b * lam + mu)

    def forward_group(n, cur, i, group, slot, between=None):
        d = group * DEEP
        near = d + 2 * core
        other = d + 2 - 2 * core
        for e in range(DEEP):
            land_rows(pp, cur * AZ + d + e, slot, i * DEEP + e)
        after = (cur + (i + 1) // GROUPS) % 2
        obs_at = jnp.maximum(n - 1, 0)
        flat_terms(pp, cur, other, terms_b, None)
        for j in range(16):
            gather_row(n, cur, i * 32 + j, obs_at)
        forward_pair(n, cur, near, terms_a)
        if between is not None:
            between()
        flat_terms(pp, after, ring_place((i + 1) % GROUPS) * DEEP + 2 * core, terms_a, None)
        for j in range(16, 32):
            gather_row(n, cur, i * 32 + j, obs_at)
        forward_pair(n, cur, other, terms_b)
        for e in range(DEEP):
            stage_rows(pp, (1 - cur) * AZ + d + e, 1 - cur, i * DEEP + e)

    flat_terms(pp, 0, ring_place(0) * DEEP + 2 * core, terms_a, None)
    observed_load.wait()
    for i in range(1, 8):
        loads[i].wait()
    wait_recv(functools.partial(whole, 3, 0))
    got_sib.wait_recv()

    def first_group(i, carry):
        @pl.when(i == 1)
        def _():
            got_up0.wait_recv()
            hop_up.start()
            pass_up0.start()
            got_down0.wait_recv()
            hop_down.start()
            pass_down0.start()
            got_up1.wait_recv()
            pass_up1.start()
            got_down1.wait_recv()
            pass_down1.start()
            via_down0.wait_recv()
            via_down1.wait_recv()

        @pl.when(i == 2)
        def _():
            via_up0.wait_recv()
            via_up1.wait_recv()

        @pl.when(i == 3)
        def _():
            got_hop_up.wait_recv()
            pass_far0.start()
            got_hop_down.wait_recv()
            pass_far1.start()

        group = ring_place(i)
        d = group * DEEP

        def passed_on():
            @pl.when(i == 3)
            def _():
                via_far0.wait_recv()
                via_far1.wait_recv()

        forward_group(0, 0, i, group, 3, passed_on)
        ready(1, i)
        scaled_pair(d)
        scaled_pair(d + 2)
        for e in range(DEEP):
            stage_rows(ff, d + e, 4, i * DEEP + e)
        ready(4, i)
        return carry

    lax.fori_loop(0, GROUPS, first_group, 0)

    def forward_step(n, carry):
        cur = n % 2

        def one_group(i, carry):
            group = ring_place(i)
            arrived(cur, i)
            forward_group(n, cur, i, group, cur)

            @pl.when(n < STEPS - 1)
            def _():
                ready(1 - cur, i)

            return carry

        lax.fori_loop(0, GROUPS, one_group, 0)
        wait_send(functools.partial(sent, cur))
        return carry

    lax.fori_loop(1, STEPS, forward_step, 0)

    out_p = pltpu.make_async_copy(pp.at[0:AZ, body], fwd_final.at[0, 0], out_sem.at[0])
    out_q = pltpu.make_async_copy(qq.at[2 : AZ + 2], fwd_final.at[0, 1], out_sem.at[1])
    out_p.start()
    out_q.start()

    def gather_last(i, carry):
        for j in range(16):
            gather_row(STEPS, 0, i * 16 + j, STEPS - 1)
        return carry

    lax.fori_loop(0, NREC // 16, gather_last, 0)

    def adj_pair(s, cur, d, terms, mode):
        nxt = 1 - cur
        here = cur * AZ + d
        there = nxt * AZ + d
        o_here = cur * (AZ + 4) + d
        o_there = nxt * (AZ + 4) + d + 2
        k = STEPS - s
        done = []
        for t in range(AX // 8):
            r = PAD + 8 * t
            at = slice(8 * t, 8 * t + 8)
            layers = [oo[o_here + n, at] for n in range(6)]
            for e in range(2):
                lam = ll[here + e, at]
                mu = mm[here + e, at]
                lam_old = ll[there + e, at]
                mu_old = mm[there + e, at]
                mix = terms[e * AX + 8 * t : e * AX + 8 * t + 8]
                lam_new = (lam + lam) - lam_old + lap(ff, here + e, r) + mix
                mu_new = (mu + mu) - mu_old + deep(layers[e : e + 5])
                done.append((ll, there + e, at, lam_new))
                done.append((mm, there + e, at, mu_new))
                if mode != "last":
                    c = cf[0, d + e, at]
                    a = cf[1, d + e, at]
                    b = cf[2, d + e, at]
                    done.append((ff, there + e, slice(r, r + 8), c * (a * lam_new + b * mu_new)))
                    done.append((oo, o_there + e, at, c * (b * lam_new + mu_new)))
                if mode != "plain":
                    h0 = hs[(k - 1) * AZ + d + e, at]
                    z0 = zs[(k - 1) * AZ + d + e, at]
                    h1 = hs[k * AZ + d + e, at]
                    z1 = zs[k * AZ + d + e, at]
                    h2 = hs[(k + 1) * AZ + d + e, at]
                    z2 = zs[(k + 1) * AZ + d + e, at]
                    q_h = lam_new * h0 + lam * h1 + lam_old * h2
                    q_x = (lam_new * z0 + mu_new * h0) + (lam * z1 + mu * h1) + (lam_old * z2 + mu_old * h2)
                    q_z = mu_new * z0 + mu * z1 + mu_old * z2
                    if mode == "last":
                        q_h += acc[0, d + e, at]
                        q_x += acc[1, d + e, at]
                        q_z += acc[2, d + e, at]
                    done.append((acc.at[0], d + e, at, q_h))
                    done.append((acc.at[1], d + e, at, q_x))
                    done.append((acc.at[2], d + e, at, q_z))
            flush(done, t)

    def set_spread(k, side):
        value = gath[k]
        high = value.astype(jnp.bfloat16)
        low = (value - high.astype(F32)).astype(jnp.bfloat16)
        base = pl.multiple_of(side * 4 * NREC, 4 * NREC)
        spread[pl.ds(base, 2 * NREC)] = jnp.concatenate([high, low], axis=0)

    def last_place(i):
        return (chip + 2 + i - 3 * (i // 2) - 2 * (i // 3)) % GROUPS

    def adj_group(s, cur, i, mode, place, between=None):
        group = place(i)
        d = group * DEEP
        slot = 4 + cur
        order = i if place is ring_place else GROUPS - 1 - i

        @pl.when(i % PER == 0)
        def _():
            wait_recv(functools.partial(halo, slot, order // PER))

        for e in range(DEEP):
            land_rows(ff, cur * AZ + d + e, slot, order * DEEP + e)
        lead = 2 - 2 * core
        flat_terms(ff, cur, d + 2 * core, terms_b, cur)
        adj_pair(s, cur, d + lead, terms_a, mode)
        if between is not None:
            between()
        flat_terms(ff, cur, place((i + 1) % GROUPS) * DEEP + lead, terms_a, cur)
        adj_pair(s, cur, d + 2 * core, terms_b, mode)
        if mode != "last":
            for e in range(DEEP):
                stage_rows(ff, (1 - cur) * AZ + d + e, 5 - cur, i * DEEP + e)
            ready(5 - cur, i)

    def adj_step(s, mode, carry):
        cur = s % 2
        set_spread(STEPS - s, cur)
        flat_terms(ff, cur, ring_place(0) * DEEP + 2 - 2 * core, terms_a, cur)

        def one_group(i, carry):
            adj_group(s, cur, i, mode, ring_place)
            return carry

        lax.fori_loop(0, GROUPS, one_group, 0)
        wait_send(functools.partial(sent, 4 + cur))
        return carry

    lax.fori_loop(0, 2, lambda s, carry: adj_step(s, "plain", carry), 0)
    adj_step(2, "third", 0)
    lax.fori_loop(3, 5, lambda s, carry: adj_step(s, "plain", carry), 0)

    def exchange(i, group):
        layer = group * DEEP
        return pltpu.make_async_remote_copy(
            src_ref=acc.at[:, pl.ds(layer + 2 * (1 - core), 2)],
            dst_ref=rb.at[:, pl.ds(2 * i, 2)],
            send_sem=rs_send.at[i],
            recv_sem=rs_recv.at[i],
            device_id=(sibling, tile),
            device_id_type=MESH,
        )

    def ring(index, layer, target):
        return pltpu.make_async_remote_copy(
            src_ref=acc.at[:, pl.ds(layer, 1)],
            dst_ref=ry.at[:, pl.ds(index, 1)],
            send_sem=rs_send.at[4 + index],
            recv_sem=rs_recv.at[4 + index],
            device_id=(target, tile),
            device_id_type=MESH,
        )

    def add_pair(i, group):
        layer = group * DEEP + 2 * core

        def add(t, carry):
            at = pl.ds(pl.multiple_of(t * 16, 16), 16)
            for f in range(3):
                for e in range(2):
                    acc[f, layer + e, at] = acc[f, layer + e, at] + rb[f, 2 * i + e, at]
            return carry

        lax.fori_loop(0, AX // 16, add, 0)

    def add_hop(index, layer):
        def add(t, carry):
            at = pl.ds(pl.multiple_of(t * 16, 16), 16)
            for f in range(3):
                acc[f, layer, at] = acc[f, layer, at] + ry[f, index, at]
            return carry

        lax.fori_loop(0, AX // 16, add, 0)

    to_up0 = ring(0, far, up)
    to_down0 = ring(1, far + 1, down)
    to_up1 = ring(2, above + 1, up)
    to_down1 = ring(3, below, down)
    to_up2 = ring(4, above, up)
    to_down2 = ring(5, below + 1, down)

    set_spread(1, 1)
    flat_terms(ff, 1, last_place(0) * DEEP + 2 - 2 * core, terms_a, 1)

    def swap(i):
        return exchange(i, last_place(i))

    def summed(i):
        swap(i).wait_send()
        swap(i).wait_recv()
        add_pair(i, last_place(i))

    def last_group(i, carry):
        adj_group(5, 1, i, "last", last_place, lambda: swap(i).start())
        summed(i)

        @pl.when(i == 0)
        def _():
            to_up0.start()
            to_down0.start()

        @pl.when(i == 1)
        def _():
            to_down1.start()

        @pl.when(i == 2)
        def _():
            to_up1.start()

        return carry

    lax.fori_loop(0, GROUPS, last_group, 0)
    out_l = pltpu.make_async_copy(ll.at[0:AZ], adj_final.at[0, 0], out_sem.at[2])
    out_m = pltpu.make_async_copy(mm.at[0:AZ], adj_final.at[0, 1], out_sem.at[3])
    out_l.start()
    out_m.start()
    to_up0.wait_recv()
    add_hop(0, above)
    to_up2.start()
    to_down0.wait_recv()
    add_hop(1, below + 1)
    to_down2.start()
    to_up1.wait_recv()
    to_down1.wait_recv()
    to_up2.wait_recv()
    to_down2.wait_recv()

    def finish(t, carry):
        at = pl.ds(pl.multiple_of(t * 16, 16), 16)
        for e, (direct, passed) in enumerate(((3, 4), (2, 5))):
            q_h, q_x, q_z = (
                acc[f, mine + e, at] + ry[f, direct, at] + ry[f, passed, at] for f in range(3)
            )
            c = cf[0, mine + e, at]
            a = cf[1, mine + e, at]
            b = cf[2, mine + e, at]
            gradient[0, e, at] = (a * q_h + b * q_x + q_z) * F32(1.0 / 12.0)
            gradient[1, e, at] = c * q_h
            gradient[2, e, at] = c * q_x
        return carry

    lax.fori_loop(0, AX // 16, finish, 0)

    for copy in (send_up0, send_down0, send_up1, send_down1, send_sib, hop_up, hop_down):
        copy.wait_send()
    for copy in (pass_up0, pass_down0, pass_up1, pass_down1, pass_far0, pass_far1):
        copy.wait_send()
    for copy in (to_up0, to_down0, to_up1, to_down1, to_up2, to_down2):
        copy.wait_send()
    wait_send(functools.partial(whole, 3, 0))
    wait_send(functools.partial(sent, 5))
    out_p.wait()
    out_q.wait()
    out_l.wait()
    out_m.wait()


def solution(mesh):
    n_shot, n_tile = mesh.shape["shot"], mesh.shape["tile"]

    def per_device(coefs, fwd_state, adj_state, src_cell, src_wave, rec_cells, observed):
        hbm = pl.BlockSpec(memory_space=pltpu.HBM)
        smem = pl.BlockSpec(memory_space=pltpu.SMEM)
        vmem = pl.BlockSpec(memory_space=pltpu.VMEM)
        dma = pltpu.SemaphoreType.DMA
        return pl.pallas_call(
            functools.partial(kernel, n_shot, n_tile),
            out_shape=(
                pltpu.VMEM((3, 2, AX, AY), F32),
                pltpu.VMEM((1, 2, AZ, AX, AY), F32),
                pltpu.VMEM((1, 2, AZ, AX, AY), F32),
            ),
            in_specs=[hbm, hbm, hbm, smem, smem, smem, vmem, hbm],
            out_specs=(vmem, vmem, vmem),
            scratch_shapes=[
                pltpu.VMEM((3, AZ, AX, AY), F32),
                pltpu.VMEM((2 * AZ, AX + 2 * PAD, AY), F32),
                pltpu.VMEM((2 * (AZ + 4), AX, AY), F32),
                pltpu.VMEM((STEPS * AZ, AX, AY), F32),
                pltpu.VMEM((STEPS * AZ, AX, AY), F32),
                pltpu.VMEM((2 * AZ, AX, AY), F32),
                pltpu.VMEM((2 * AZ, AX, AY), F32),
                pltpu.VMEM((2 * AZ, AX + 2 * PAD, AY), F32),
                pltpu.VMEM((2 * (AZ + 4), AX, AY), F32),
                pltpu.VMEM((3, AZ, AX, AY), F32),
                pltpu.VMEM((3, 8, AX, AY), F32),
                pltpu.VMEM((3, 6, AX, AY), F32),
                pltpu.VMEM((2 * 192, AY), F32),
                pltpu.VMEM((2 * 192, AY), F32),
                pltpu.VMEM((AZ * AX, 2 * NREC), jnp.bfloat16),
                pltpu.VMEM((STEPS + 1, NREC, AY), F32),
                pltpu.VMEM((8 * NREC, AY), jnp.bfloat16),
                pltpu.VMEM((2 * AX, AY), F32),
                pltpu.VMEM((2 * AX, AY), F32),
                pltpu.SMEM((STEPS, 1, NREC), F32),
                dma((10,)),
                dma((4,)),
                dma((2, 6)),
                dma((2, 6, 4)),
                dma((2, 1)),
                dma((2, 1)),
                dma((13,)),
                dma((13,)),
                dma((10,)),
                dma((10,)),
            ],
            compiler_params=pltpu.CompilerParams(
                collective_id=0, has_side_effects=True, vmem_limit_bytes=56 * 1024 * 1024
            ),
        )(coefs, fwd_state, adj_state, src_cell, src_wave, rec_cells, rec_cells, observed.transpose(1, 0, 2))

    placed = (
        P(None, "shot", "tile", None),
        P("shot", None, None, "tile", None),
        P("shot", None, None, "tile", None),
        P("shot", "tile"),
        P("shot", None),
        P("shot", "tile"),
        P("shot", None, "tile"),
    )
    return jax.shard_map(
        per_device,
        mesh=mesh,
        in_specs=placed,
        out_specs=(
            P(None, "shot", "tile", None),
            P("shot", None, None, "tile", None),
            P("shot", None, None, "tile", None),
        ),
        check_vma=False,
    )
```
